512 devices in a mesh: outer: 64 (over x_hi, z, core), inner: 8 (over y, x_lo).
Axes of the slice: x: 4 (x_hi: 2, x_lo: 2; x = x_hi * 2 + x_lo), y: 4, z: 16, core: 2. Of those that a mesh axis runs over, the one named last changes fastest.
Arguments:
- queries: bfloat16 [196608, 256], P(('outer', 'inner')), may hold values from -20 to 20
- key_rows: bfloat16 [196608, 256], P(('outer', 'inner')), may hold values from -20 to 20
- value_rows: bfloat16 [196608, 256], P(('outer', 'inner')), may hold values from -6 to 6
- outputs: bfloat16 [196608, 256], P(('outer', 'inner')), may hold values from -4 to 4
- out_grad: bfloat16 [196608, 256], P(('outer', 'inner')), may hold values from -6 to 6
Outputs:
- query_grad: bfloat16 [196608, 256], P(('outer', 'inner'))
- key_grad: bfloat16 [196608, 256], P(('outer', 'inner'))
- value_grad: bfloat16 [196608, 256], P(('outer', 'inner'))
The draws below stay inside these ranges and needn't reach their ends.
All inputs are finite; a program needn't handle non-finite values.
Results may differ from the reference program's by a relative error of at most 0.014.
Values may be sent and summed in bfloat16 or wider, within the bound.
No kernel may reach another device: no remote copies, remote signals or barrier semaphores. Data moves between devices by JAX's collectives and lax.ppermute only.
A program may use at most 64 MiB of HBM per device.

```python
import jax
import jax.numpy as jnp
from jax import lax

HEADS = 2
HEAD_DIM = 128
BLOCK = 3072
TOKENS = 196608
N_OUTER = 64


def draw_queries(key, part):
    key = jax.random.fold_in(key, 11)
    fresh = jax.random.truncated_normal(key, -4.5, 4.5, (TOKENS, HEADS * HEAD_DIM), jnp.float32)
    return fresh.astype(jnp.bfloat16)


def draw_key_rows(key, part):
    key = jax.random.fold_in(key, 12)
    fresh = jax.random.truncated_normal(key, -4.5, 4.5, (TOKENS, HEADS * HEAD_DIM), jnp.float32)
    return fresh.astype(jnp.bfloat16)


def block_scale(own_key, shape, cuts, smallest, top_value):
    gain, own = 1.0, jax.random.fold_in(own_key, 6)
    for dim, shards_of in cuts:
        draws = jnp.exp(jax.random.uniform(jax.random.fold_in(own, dim), (shards_of,), jnp.float32, smallest / len(cuts), top_value / len(cuts)))
        gain = gain * jnp.repeat(draws, shape[dim] // shards_of).reshape([-1 if axis == dim else 1 for axis in range(len(shape))])
    return gain


def bell_draw(rng, shape, spread, most, pieces=(), kind=jnp.bfloat16):
    gain = block_scale(rng, shape, pieces, -0.22, 0.18) if pieces else 1.0
    drawn = jax.random.normal(rng, shape, jnp.float32) * spread * gain
    return jnp.minimum(jnp.maximum(drawn, -most), most).astype(kind)


def setup_inputs(seed: int = 0) -> dict:
    streams_of = jax.random.split(jax.random.key(seed), 6)
    return {
        "queries": draw_queries(jax.random.fold_in(streams_of[5], 71), 0),
        "key_rows": draw_key_rows(jax.random.fold_in(streams_of[5], 71), 0),
        "value_rows": bell_draw(streams_of[2], (TOKENS, HEADS * HEAD_DIM), 1.0, 6.0, ((0, 512),)),
        "outputs": bell_draw(streams_of[3], (TOKENS, HEADS * HEAD_DIM), 0.5, 4.0, ((0, 512),)),
        "out_grad": bell_draw(streams_of[4], (TOKENS, HEADS * HEAD_DIM), 1.0, 6.0, ((0, 512),)),
    }


def heads_wide(block):
    return block.astype(jnp.float32).reshape(block.shape[0], HEADS, HEAD_DIM)


def reference(queries, key_rows, value_rows, outputs, out_grad):
    scale_factor = HEAD_DIM ** -0.5

    def rows_of(array, index):
        start = (index * BLOCK).astype(jnp.int32)
        return lax.dynamic_slice_in_dim(array, start, BLOCK, 0)

    def one_block(index):
        prior = ((index + N_OUTER - 1) % N_OUTER).astype(jnp.int32)
        query_heads = heads_wide(rows_of(queries, index))
        grad_heads = heads_wide(rows_of(out_grad, index))
        output_heads = heads_wide(rows_of(outputs, index))
        key_heads = heads_wide(jnp.concatenate([rows_of(key_rows, index), rows_of(key_rows, prior)], axis=0))
        value_heads = heads_wide(jnp.concatenate([rows_of(value_rows, index), rows_of(value_rows, prior)], axis=0))
        scores = jnp.einsum("qhd,khd->hqk", query_heads, key_heads) * scale_factor
        largest = jnp.max(scores, axis=2)
        lse_rows = largest + jnp.log(jnp.sum(jnp.exp(scores - largest[:, :, None]), axis=2))
        weights = jnp.exp(scores - lse_rows[:, :, None])
        weights_low = weights.astype(jnp.bfloat16).astype(jnp.float32)
        delta_rows = jnp.einsum("qhd,qhd->hq", grad_heads, output_heads)
        prob_grad = jnp.einsum("qhd,khd->hqk", grad_heads, value_heads)
        score_grad = (weights * (prob_grad - delta_rows[:, :, None]) * scale_factor).astype(jnp.bfloat16).astype(jnp.float32)
        grad_query = jnp.einsum("hqk,khd->qhd", score_grad, key_heads).reshape(BLOCK, HEADS * HEAD_DIM)
        grad_key = jnp.einsum("hqk,qhd->khd", score_grad, query_heads).reshape(2 * BLOCK, HEADS * HEAD_DIM)
        grad_value = jnp.einsum("hqk,qhd->khd", weights_low, grad_heads).reshape(2 * BLOCK, HEADS * HEAD_DIM)
        return grad_query, grad_key, grad_value

    grads = lax.map(one_block, jnp.arange(N_OUTER, dtype=jnp.int32))
    query_grad = grads[0].reshape(TOKENS, HEADS * HEAD_DIM)
    key_total = grads[1][:, :BLOCK] + jnp.roll(grads[1][:, BLOCK:], -1, axis=0)
    value_total = grads[2][:, :BLOCK] + jnp.roll(grads[2][:, BLOCK:], -1, axis=0)
    key_grad = key_total.reshape(TOKENS, HEADS * HEAD_DIM)
    value_grad = value_total.reshape(TOKENS, HEADS * HEAD_DIM)
    return query_grad.astype(jnp.bfloat16), key_grad.astype(jnp.bfloat16), value_grad.astype(jnp.bfloat16)
```

```python
import functools

import jax
import jax.numpy as jnp
from jax import lax
from jax.experimental import pallas as pl
from jax.experimental.pallas import tpu as pltpu
from jax.sharding import PartitionSpec as P

R = 384
D = 128
SCALE = D ** -0.5
C = SCALE * 1.4426950408889634
NK = 1536
F32 = jnp.float32
BF = jnp.bfloat16
MB = 1024 * 1024
VM = pl.BlockSpec(memory_space=pltpu.VMEM)


def dot(a, b, ca, cb):
    return lax.dot_general(a, b, (((ca,), (cb,)), ((), ())), preferred_element_type=F32)


def params(mb):
    return pltpu.CompilerParams(vmem_limit_bytes=mb * MB)


def prep_body(q, k, v, o, g, qg, kv):
    def t(x):
        return x[...].astype(F32).T
    gt = t(g)
    qg[0:256] = t(q).astype(BF)
    qg[256:512] = gt.astype(BF)
    kv[0:256] = t(k).astype(BF)
    kv[256:512] = t(v).astype(BF)
    prod = gt * t(o)
    parts = []
    for h in range(2):
        d = jnp.sum(prod[h * D:(h + 1) * D], axis=0, keepdims=True)
        hi = d.astype(BF).astype(F32)
        mid = (d - hi).astype(BF).astype(F32)
        parts += [hi, mid, d - hi - mid]
    qg[512:528] = jnp.concatenate(parts + [jnp.zeros((10, R), F32)], axis=0).astype(BF)


def prep(q, k, v, o, g):
    return pl.pallas_call(
        prep_body,
        out_shape=[jax.ShapeDtypeStruct((528, R), BF), jax.ShapeDtypeStruct((512, R), BF)],
        name="pack",
    )(q, k, v, o, g)


def gather_keys(dst, refs, h, base):
    for n, ref in enumerate(refs):
        dst[h, 0:D, n * R:(n + 1) * R] = ref[base + h * D:base + (h + 1) * D, :]


def k1_body(*refs):
    qg, kv = refs[0:4], refs[4:8]
    p_ref, st_ref, ks, st = refs[8:]
    for h in range(2):
        gather_keys(ks, kv, h, 0)
    for n in range(4):
        for h in range(2):
            s = dot(qg[n][h * D:(h + 1) * D, :], ks[h], 0, 0)
            m = jnp.max(s, axis=1, keepdims=True) * C
            p = jnp.exp2(s * C - m)
            st[n * R:(n + 1) * R, 2 * h:2 * h + 1] = m
            st[n * R:(n + 1) * R, 2 * h + 1:2 * h + 2] = jnp.sum(p, axis=1, keepdims=True)
            p_ref[h, n * R:(n + 1) * R, :] = p.astype(BF)
    st_ref[...] = st[...].T[0:8, :]


BIG = pltpu.VMEM((2, 1536, NK), BF)


def stage1(qg, kv):
    return pl.pallas_call(
        k1_body,
        in_specs=[VM] * 8,
        out_specs=[VM, VM],
        out_shape=[BIG, jax.ShapeDtypeStruct((8, 1536), F32)],
        scratch_shapes=[pltpu.VMEM((2, D, NK), BF), pltpu.VMEM((1536, D), F32)],
        compiler_params=params(30),
        name="scores",
    )(*qg, *kv)


def k2_body(*refs):
    qg, kv, p_ref, ds_ref = refs[0:4], refs[4:8], refs[8], refs[9]
    out = refs[10:14]
    ks, vs, gs = refs[14:]
    row = lax.broadcasted_iota(jnp.int32, (16, NK), 0)
    for h in range(2):
        gather_keys(ks, kv, h, 0)
        gather_keys(vs, kv, h, 256)
        vs[h, D:D + 16, :] = jnp.where((row >= 3 * h) & (row < 3 * h + 3), -1.0, 0.0).astype(BF)
    for n in range(4):
        for h in range(2):
            gs[n, h, 0:D, :] = qg[n][256 + h * D:256 + (h + 1) * D, :]
            gs[n, h, D:D + 16, :] = qg[n][512:528, :]
            pg = dot(gs[n, h], vs[h], 0, 0)
            ds = (p_ref[h, n * R:(n + 1) * R, :].astype(F32) * pg).astype(BF)
            ds_ref[h, n * R:(n + 1) * R, :] = ds
            out[n][:, h * D:(h + 1) * D] = dot(ds, ks[h], 1, 1).astype(BF)


def stage2(qg, kv, p):
    return pl.pallas_call(
        k2_body,
        in_specs=[VM] * 9,
        out_specs=[VM] * 5,
        out_shape=[BIG] + [jax.ShapeDtypeStruct((R, 2 * D), BF)] * 4,
        scratch_shapes=[pltpu.VMEM((2, D, NK), BF), pltpu.VMEM((2, D + 16, NK), BF), pltpu.VMEM((4, 2, D + 16, R), BF)],
        compiler_params=params(30),
        name="score_grads",
    )(*qg, *kv, p)


REL = (0, 1, 3, 2)


def chunk_of(sender, n):
    return REL.index((REL[n] - REL[sender]) % 4)


def factors(stats, h, n):
    ms, ls = [], []
    for sender, ref in enumerate(stats):
        c = chunk_of(sender, n)
        ms.append(ref[2 * h:2 * h + 1, c * R:(c + 1) * R])
        ls.append(ref[2 * h + 1:2 * h + 2, c * R:(c + 1) * R])
    top = functools.reduce(jnp.maximum, ms)
    scaled = [jnp.exp2(m - top) for m in ms]
    total = sum(l * e for l, e in zip(ls, scaled))
    return [e / total for e in scaled]


def k3_body(*refs):
    qg, st, p_ref, ds_ref = refs[0:4], refs[4:8], refs[8], refs[9]
    prior, own = refs[10:12]
    xs = refs[12]
    for h in range(2):
        for n in range(4):
            fn = factors(st, h, n)[0]
            xs[h, 0, :, n * R:(n + 1) * R] = (qg[n][h * D:(h + 1) * D, :].astype(F32) * (fn * SCALE)).astype(BF)
            xs[h, 1, :, n * R:(n + 1) * R] = (qg[n][256 + h * D:256 + (h + 1) * D, :].astype(F32) * fn).astype(BF)
    for out, cols in ((prior, slice(768, 1536)), (own, slice(0, 768))):
        for h in range(2):
            out[h * D:(h + 1) * D, :] = dot(xs[h, 0], ds_ref[h, :, cols], 1, 0).astype(out.dtype)
            out[256 + h * D:256 + (h + 1) * D, :] = dot(xs[h, 1], p_ref[h, :, cols], 1, 0).astype(out.dtype)


def stage3(qg, stats, p, ds):
    return pl.pallas_call(
        k3_body,
        in_specs=[VM] * 10,
        out_specs=[VM] * 2,
        out_shape=[jax.ShapeDtypeStruct((512, 768), BF), jax.ShapeDtypeStruct((512, 768), F32)],
        scratch_shapes=[pltpu.VMEM((2, 2, D, 1536), BF)],
        compiler_params=params(30),
        name="key_grads",
    )(*qg, *stats, p, ds)


def query_sum_body(a0, a1, a2, a3, s0, s1, s2, s3, out):
    parts = (a0, a1, a2, a3)
    rows = []
    for h in range(2):
        rows += factors((s0, s1, s2, s3), h, 0)
    cols = jnp.concatenate(rows, axis=0).T
    for h in range(2):
        cut = slice(h * D, (h + 1) * D)
        total = sum(parts[n][:, cut].astype(F32) * cols[:, 4 * h + n:4 * h + n + 1] for n in range(4))
        out[:, cut] = (total * SCALE).astype(BF)


def query_sum(parts, stats):
    return pl.pallas_call(
        query_sum_body,
        out_shape=jax.ShapeDtypeStruct((R, 2 * D), BF),
        name="query_sum",
    )(*parts, *stats)


def partner_sum_body(own, back, out):
    out[...] = (own[:, R:] + back[:, R:].astype(F32)).astype(BF)


def partner_sum(own, back):
    return pl.pallas_call(
        partner_sum_body,
        out_shape=jax.ShapeDtypeStruct((512, R), BF),
        name="partner_sum",
    )(own, back)


def key_sum_body(own, back, other, dk, dv):
    total = own[:, :R] + back[:, :R].astype(F32) + other[...].astype(F32)
    dk[...] = total[0:256].T.astype(BF)
    dv[...] = total[256:512].T.astype(BF)


def key_sum(own, back, other):
    return pl.pallas_call(
        key_sum_body,
        out_shape=[jax.ShapeDtypeStruct((R, 2 * D), BF)] * 2,
        name="key_sum",
    )(own, back, other)


def along_y(value, steps):
    pairs = [(2 * y + x, 2 * ((y + steps) % 4) + x) for y in range(4) for x in range(2)]
    return lax.ppermute(value, "inner", pairs)


def along_x(value):
    return lax.ppermute(value, "inner", [(i, i ^ 1) for i in range(8)])


def along_outer(value, steps):
    n = lax.axis_size("outer")
    return lax.ppermute(value, "outer", [(i, (i + steps) % n) for i in range(n)])


def from_peers(value):
    return [along_y(value, -REL[n]) for n in (1, 2, 3)]


def on_device(queries, key_rows, value_rows, outputs, out_grad):
    qg_own, kv_own = prep(queries, key_rows, value_rows, outputs, out_grad)
    kv_other = along_x(kv_own)
    qg = [qg_own] + from_peers(qg_own)
    kv = [kv_own, kv_other, along_outer(kv_own, 1), along_outer(kv_other, 1)]
    p, st = stage1(qg, kv)
    stats = [st] + from_peers(st)
    ds, *parts = stage2(qg, kv, p)
    parts = [parts[0]] + [along_y(parts[REL.index(-REL[n] % 4)], -REL[n]) for n in (1, 2, 3)]
    prior, own = stage3(qg, stats, p, ds)
    back = along_outer(prior, -1)
    other = along_x(partner_sum(own, back))
    query_grad = query_sum(parts, stats)
    key_grad, value_grad = key_sum(own, back, other)
    return query_grad, key_grad, value_grad


def solution(mesh):
    spec = P(("outer", "inner"), None)
    return jax.shard_map(
        on_device, mesh=mesh, in_specs=(spec,) * 5, out_specs=(spec,) * 3, check_vma=False
    )
```

```python
import jax
import jax.numpy as jnp
from jax import lax
from jax.experimental import pallas as pl
from jax.experimental.pallas import tpu as pltpu
from jax.sharding import PartitionSpec as P

R = 384
D = 128
SCALE = D ** -0.5
C = SCALE * 1.4426950408889634
NQ = 4 * R
NK = 4 * R
F32 = jnp.float32
BF = jnp.bfloat16
VM = pl.BlockSpec(memory_space=pltpu.VMEM)
HBM = pl.BlockSpec(memory_space=pltpu.HBM)
PARAMS = pltpu.CompilerParams(vmem_limit_bytes=16 * 1024 * 1024)
ALONE = pltpu.CompilerParams(vmem_limit_bytes=60 * 1024 * 1024)


def dot(a, b, ca, cb):
    return lax.dot_general(a, b, (((ca,), (cb,)), ((), ())), preferred_element_type=F32)


def chunk(n):
    return slice(n * R, (n + 1) * R)


def head(h, base=0):
    return slice(base + h * D, base + (h + 1) * D)


def turned(copies, refs, n):
    copies[n].wait()
    return refs[n][...].astype(F32).T


def started(refs, held, sems):
    copies = [pltpu.make_async_copy(ref, held[n], sems.at[n]) for n, ref in enumerate(refs)]
    for copy in copies:
        copy.start()
    return copies


def pack_keys_body(k, v, kv, ks, vs, sems):
    held = (ks, vs)
    copies = started((k, v), held, sems)
    kv[0:256] = turned(copies, held, 0).astype(BF)
    kv[256:512] = turned(copies, held, 1).astype(BF)
    kv[512:544] = jnp.zeros((32, R), BF)


def pack_queries_body(q, o, g, qg, qs, os, gs, sems):
    held = (qs, os, gs)
    copies = started((q, o, g), held, sems)
    qg[0:256] = turned(copies, held, 0).astype(BF)
    outs = turned(copies, held, 1)
    grads = turned(copies, held, 2)
    qg[256:512] = grads.astype(BF)
    prod = grads * outs
    rows = []
    for h in range(2):
        d = jnp.sum(prod[head(h)], axis=0, keepdims=True)
        hi = d.astype(BF).astype(F32)
        mid = (d - hi).astype(BF).astype(F32)
        rows += [hi, mid, d - hi - mid]
    qg[512:528] = jnp.concatenate(rows + [jnp.zeros((10, R), F32)], axis=0).astype(BF)


def pack_keys(k, v):
    return pl.pallas_call(
        pack_keys_body,
        in_specs=[HBM] * 2,
        out_specs=VM,
        out_shape=pltpu.VMEM((544, R), BF),
        scratch_shapes=[pltpu.VMEM((R, 2 * D), BF)] * 2 + [pltpu.SemaphoreType.DMA((2,))],
        compiler_params=ALONE,
        name="pack_keys",
    )(k, v)


def pack_queries(q, o, g):
    return pl.pallas_call(
        pack_queries_body,
        in_specs=[HBM] * 3,
        out_specs=VM,
        out_shape=pltpu.VMEM((528, R), BF),
        scratch_shapes=[pltpu.VMEM((R, 2 * D), BF)] * 3 + [pltpu.SemaphoreType.DMA((3,))],
        compiler_params=ALONE,
        name="pack_queries",
    )(q, o, g)


def scores_body(*refs):
    qg, kv = refs[0:4], refs[4:8]
    p_ref, st_ref, ks, st = refs[8:]
    for h in range(2):
        for n in range(4):
            ks[h, :, chunk(n)] = kv[n][head(h), :]
    for n in range(4):
        for h in range(2):
            s = dot(qg[n][head(h), :], ks[h], 0, 0)
            m = jnp.max(s, axis=1, keepdims=True) * C
            p = jnp.exp2(s * C - m)
            st[chunk(n), h:h + 1] = m
            st[chunk(n), 2 + h:3 + h] = jnp.sum(p, axis=1, keepdims=True)
            p_ref[h, chunk(n), :] = p.astype(BF)
    st_ref[...] = st[...].T[0:8, :]


def scores(qg, kv):
    return pl.pallas_call(
        scores_body,
        in_specs=[VM] * 8,
        out_specs=[VM] * 2,
        out_shape=[pltpu.VMEM((2, NQ, NK), BF), pltpu.VMEM((8, NQ), F32)],
        scratch_shapes=[pltpu.VMEM((2, D, NK), BF), pltpu.VMEM((NQ, D), F32)],
        compiler_params=PARAMS,
        name="scores",
    )(*qg, *kv)


def merged(a, b, m):
    b = jnp.concatenate([b[0:4, chunk(n ^ m)] for n in range(4)], axis=1)
    top = jnp.maximum(a[0:2], b[0:2])
    total = a[2:4] * jnp.exp2(a[0:2] - top) + b[2:4] * jnp.exp2(b[0:2] - top)
    return top, total


def merge_body(a, b, after, out):
    top, total = merged(a[...], b[...], 1)
    out[0:2] = top
    out[2:4] = total
    out[4:8] = jnp.zeros((4, NQ), F32)


def merge(a, b, after):
    return pl.pallas_call(
        merge_body,
        in_specs=[VM] * 3,
        out_specs=VM,
        out_shape=pltpu.VMEM((8, NQ), F32),
        compiler_params=PARAMS,
        name="merge",
    )(a, b, after)


def score_grads_body(h, *refs):
    qg, kv, p_ref = refs[0:4], refs[4:8], refs[8]
    ds_ref, dq_ref, ks, vs, gs = refs[9:]
    row = lax.broadcasted_iota(jnp.int32, (16, NK), 0)
    for n in range(4):
        ks[:, chunk(n)] = kv[n][head(h), :]
        vs[0:D, chunk(n)] = kv[n][head(h, 256), :]
        gs[n, 0:D, :] = qg[n][head(h, 256), :]
        gs[n, D:D + 16, :] = qg[n][512:528, :]
    vs[D:D + 16, :] = jnp.where((row >= 3 * h) & (row < 3 * h + 3), -1.0, 0.0).astype(BF)
    for n in range(4):
        pg = dot(gs[n], vs[...], 0, 0)
        ds = (p_ref[h, chunk(n), :].astype(F32) * pg).astype(BF)
        ds_ref[chunk(n), :] = ds
        dq_ref[chunk(n), :] = dot(ds, ks[...], 1, 1)


def score_grads(h, qg, kv, p):
    return pl.pallas_call(
        lambda *refs: score_grads_body(h, *refs),
        in_specs=[VM] * 9,
        out_specs=[VM] * 2,
        out_shape=[pltpu.VMEM((NQ, NK), BF), pltpu.VMEM((NQ, D), F32)],
        scratch_shapes=[
            pltpu.VMEM((D, NK), BF),
            pltpu.VMEM((D + 16, NK), BF),
            pltpu.VMEM((4, D + 16, R), BF),
        ],
        compiler_params=PARAMS,
        name="score_grads",
    )(*qg, *kv, p)


def key_part(out, xs, ds, p_ref, cols):
    for h in range(2):
        out[head(h), :] = dot(xs[h, 0], ds[h][:, cols], 1, 0).astype(out.dtype)
        out[head(h, 256), :] = dot(xs[h, 1], p_ref[h, :, cols], 1, 0).astype(out.dtype)


def prior_partner_body(*refs):
    qg, own, pair, other, p_ref, ds, dqs = refs[0:4], refs[4], refs[5], refs[6], refs[7], refs[8:10], refs[10:12]
    out, xs, near, far = refs[12:]
    top, total = merged(pair[...], other[...], 3)
    f = jnp.exp2(own[0:2] - top) / total
    cols = jnp.concatenate([f * SCALE, jnp.zeros((6, NQ), F32)], axis=0).T
    for place, n in ((0, 0), (1, 1)):
        for h, dq in enumerate(dqs):
            near[chunk(place), head(h)] = dq[chunk(n), :] * cols[chunk(n), h:h + 1]
    for place, n in ((0, 3), (1, 2)):
        for h, dq in enumerate(dqs):
            far[chunk(place), head(h)] = (dq[chunk(n), :] * cols[chunk(n), h:h + 1]).astype(BF)
    for h in range(2):
        for n in range(4):
            fn = f[h:h + 1, chunk(n)]
            xs[h, 0, :, chunk(n)] = (qg[n][head(h), :].astype(F32) * (fn * SCALE)).astype(BF)
            xs[h, 1, :, chunk(n)] = (qg[n][head(h, 256), :].astype(F32) * fn).astype(BF)
    key_part(out, xs, ds, p_ref, chunk(3))


def prior_partner(qg, own, pair, other, p, ds, dq):
    return pl.pallas_call(
        prior_partner_body,
        in_specs=[VM] * 12,
        out_specs=[VM] * 4,
        out_shape=[
            pltpu.VMEM((512, R), BF),
            pltpu.VMEM((2, 2, D, NQ), BF),
            pltpu.VMEM((2 * R, 2 * D), F32),
            pltpu.VMEM((2 * R, 2 * D), BF),
        ],
        compiler_params=PARAMS,
        name="prior_partner",
    )(*qg, own, pair, other, p, *ds, *dq)


def key_grads_body(xs, p_ref, ds0, ds1, own_partner, prior, own):
    ds = (ds0, ds1)
    key_part(own_partner, xs, ds, p_ref, chunk(1))
    key_part(prior, xs, ds, p_ref, chunk(2))
    key_part(own, xs, ds, p_ref, chunk(0))


def key_grads(xs, p, ds):
    part = pltpu.VMEM((512, R), F32)
    return pl.pallas_call(
        key_grads_body,
        in_specs=[VM] * 4,
        out_specs=[VM] * 3,
        out_shape=[pltpu.VMEM((512, R), BF), part, part],
        compiler_params=PARAMS,
        name="key_grads",
    )(xs, p, *ds)


def prior_sum_body(a, b, out):
    out[...] = (a[...] + b[...].astype(F32)).astype(BF)


def prior_sum(a, b):
    return pl.pallas_call(
        prior_sum_body,
        in_specs=[VM] * 2,
        out_specs=VM,
        out_shape=pltpu.VMEM((512, R), BF),
        compiler_params=PARAMS,
        name="prior_sum",
    )(a, b)


def query_mid_body(near, far, own, pair):
    own[...] = near[chunk(0), :] + far[chunk(0), :].astype(F32)
    pair[...] = (near[chunk(1), :] + far[chunk(1), :].astype(F32)).astype(BF)


def query_mid(near, far):
    return pl.pallas_call(
        query_mid_body,
        in_specs=[VM] * 2,
        out_specs=[VM] * 2,
        out_shape=[pltpu.VMEM((R, 2 * D), F32), pltpu.VMEM((R, 2 * D), BF)],
        compiler_params=PARAMS,
        name="query_mid",
    )(near, far)


def query_sum_body(own, pair, out):
    out[...] = (own[...] + pair[...].astype(F32)).astype(BF)


def query_sum(own, pair):
    return pl.pallas_call(
        query_sum_body,
        in_specs=[VM] * 2,
        out_shape=jax.ShapeDtypeStruct((R, 2 * D), BF),
        compiler_params=PARAMS,
        name="query_sum",
    )(own, pair)


def key_sum_body(own, other, back, dk, dv):
    total = own[...] + other[...].astype(F32) + back[...].astype(F32)
    dk[...] = total[0:256].T.astype(BF)
    dv[...] = total[256:512].T.astype(BF)


def key_sum(own, other, back):
    return pl.pallas_call(
        key_sum_body,
        in_specs=[VM] * 3,
        out_shape=[jax.ShapeDtypeStruct((R, 2 * D), BF)] * 2,
        compiler_params=PARAMS,
        name="key_sum",
    )(own, other, back)


def along_y(value, m):
    return lax.ppermute(value, "inner", [(i, i ^ (2 * m)) for i in range(8)])


def passed_on(one, three):
    outer, inner = lax.axis_size("outer"), lax.axis_size("inner")
    pairs = [
        (o * inner + i, o * inner + (i ^ (2 if o % 2 == 0 else 6))) for o in range(outer) for i in range(inner)
    ]
    value = jnp.where(lax.axis_index("outer") % 2 == 0, three, one)
    return lax.ppermute(value, ("outer", "inner"), pairs)


def along_x(value):
    return lax.ppermute(value, "inner", [(i, i ^ 1) for i in range(8)])


def window_pairs():
    outer, inner = lax.axis_size("outer"), lax.axis_size("inner")
    turn = outer // 2
    return [
        (o * inner + i, (o + 1) % outer * inner + (i ^ 1 if o % turn == turn - 1 else i))
        for o in range(outer)
        for i in range(inner)
    ]


def to_next(value):
    return lax.ppermute(value, ("outer", "inner"), window_pairs())


def to_prior(value):
    return lax.ppermute(value, ("outer", "inner"), [(b, a) for a, b in window_pairs()])


def on_device(queries, key_rows, value_rows, outputs, out_grad):
    kv_own = pack_keys(key_rows, value_rows)
    qg_own = pack_queries(queries, outputs, out_grad)
    kv_prior = to_next(kv_own)
    kv_partner = along_x(kv_own)
    kv = [kv_own, kv_partner, kv_prior, to_next(kv_partner)]
    qg_1, qg_3 = along_y(qg_own, 1), along_y(qg_own, 3)
    qg = [qg_own, qg_1, passed_on(qg_1, qg_3), qg_3]
    p, st = scores(qg, kv)
    st_pair = along_y(st, 1)
    ds0, dq0 = score_grads(0, qg, kv, p)
    pair = merge(st, st_pair, dq0)
    pair_other = along_y(pair, 3)
    ds1, dq1 = score_grads(1, qg, kv, p)
    ds, dq = (ds0, ds1), (dq0, dq1)
    part, xs, near, far = prior_partner(qg, st, pair, pair_other, p, ds, dq)
    part = along_x(part)
    far = along_y(far, 3)
    own_partner, prior, own = key_grads(xs, p, ds)
    other = along_x(own_partner)
    back = to_prior(prior_sum(prior, part))
    near, pair = query_mid(near, far)
    query_grad = query_sum(near, along_y(pair, 1))
    key_grad, value_grad = key_sum(own, other, back)
    return query_grad, key_grad, value_grad


def solution(mesh):
    spec = P(("outer", "inner"), None)
    return jax.shard_map(
        on_device, mesh=mesh, in_specs=(spec,) * 5, out_specs=(spec,) * 3, check_vma=False
    )
```

```python
import jax
import jax.numpy as jnp
from jax import lax
from jax.experimental import pallas as pl
from jax.experimental.pallas import tpu as pltpu
from jax.sharding import PartitionSpec as P

R = 384
D = 128
SCALE = D ** -0.5
C = SCALE * 1.4426950408889634
NQ = 4 * R
NK = 4 * R
F32 = jnp.float32
BF = jnp.bfloat16
VM = pl.BlockSpec(memory_space=pltpu.VMEM)
HBM = pl.BlockSpec(memory_space=pltpu.HBM)
PARAMS = pltpu.CompilerParams(vmem_limit_bytes=16 * 1024 * 1024)
ALONE = pltpu.CompilerParams(vmem_limit_bytes=60 * 1024 * 1024)


def dot(a, b, ca, cb):
    return lax.dot_general(a, b, (((ca,), (cb,)), ((), ())), preferred_element_type=F32)


def chunk(n):
    return slice(n * R, (n + 1) * R)


def head(h, base=0):
    return slice(base + h * D, base + (h + 1) * D)


def turned(copies, refs, n):
    copies[n].wait()
    return refs[n][...].astype(F32).T


def started(refs, held, sems):
    copies = [pltpu.make_async_copy(ref, held[n], sems.at[n]) for n, ref in enumerate(refs)]
    for copy in copies:
        copy.start()
    return copies


def pack_keys_body(k, v, kv, ks, vs, sems):
    held = (ks, vs)
    copies = started((k, v), held, sems)
    kv[0:256] = turned(copies, held, 0).astype(BF)
    kv[256:512] = turned(copies, held, 1).astype(BF)


def pack_queries_body(q, o, g, qg, qs, os, gs, sems):
    held = (qs, os, gs)
    copies = started((q, o, g), held, sems)
    qg[0:256] = turned(copies, held, 0).astype(BF)
    outs = turned(copies, held, 1)
    grads = turned(copies, held, 2)
    qg[256:512] = grads.astype(BF)
    prod = grads * outs
    rows = []
    for h in range(2):
        d = jnp.sum(prod[head(h)], axis=0, keepdims=True)
        hi = d.astype(BF).astype(F32)
        mid = (d - hi).astype(BF).astype(F32)
        rows += [hi, mid, d - hi - mid]
    qg[512:528] = jnp.concatenate(rows + [jnp.zeros((10, R), F32)], axis=0).astype(BF)


def pack_keys(k, v):
    return pl.pallas_call(
        pack_keys_body,
        in_specs=[HBM] * 2,
        out_specs=VM,
        out_shape=pltpu.VMEM((512, R), BF),
        scratch_shapes=[pltpu.VMEM((R, 2 * D), BF)] * 2 + [pltpu.SemaphoreType.DMA((2,))],
        compiler_params=ALONE,
        name="pack_keys",
    )(k, v)


def pack_queries(q, o, g):
    return pl.pallas_call(
        pack_queries_body,
        in_specs=[HBM] * 3,
        out_specs=VM,
        out_shape=pltpu.VMEM((528, R), BF),
        scratch_shapes=[pltpu.VMEM((R, 2 * D), BF)] * 3 + [pltpu.SemaphoreType.DMA((3,))],
        compiler_params=ALONE,
        name="pack_queries",
    )(q, o, g)


def score_chunk(n, h, q, keys, p_ref, st):
    scaled = q[head(h), :].astype(F32) * C
    high = scaled.astype(BF)
    low = (scaled - high.astype(F32)).astype(BF)
    s = dot(jnp.concatenate([high, low], axis=0), keys, 0, 0)
    m = jnp.max(s, axis=1, keepdims=True)
    p = jnp.exp2(s - m)
    st[:, h:h + 1] = m
    st[:, 2 + h:3 + h] = jnp.sum(p, axis=1, keepdims=True)
    p_ref[h, chunk(n), :] = p.astype(BF)


def first_scores_body(own, first, k0, k1, k2, k3, p_ref, st_ref, ks, st):
    for n, ref in enumerate((k0, k1, k2, k3)):
        for h in range(2):
            ks[h, 0:D, chunk(n)] = ref[head(h), :]
            ks[h, D:2 * D, chunk(n)] = ref[head(h), :]
    for n, q in enumerate((own, first)):
        for h in range(2):
            score_chunk(n, h, q, ks[h], p_ref, st.at[n])
        st_ref[:, chunk(n)] = st[n].T[0:8, :]
    st_ref[:, 2 * R:4 * R] = jnp.zeros((8, 2 * R), F32)


def first_scores(qg, kv):
    return pl.pallas_call(
        first_scores_body,
        in_specs=[VM] * 6,
        out_specs=[VM] * 3,
        out_shape=[pltpu.VMEM((2, NQ, NK), BF), pltpu.VMEM((8, NQ), F32), pltpu.VMEM((2, 2 * D, NK), BF)],
        scratch_shapes=[pltpu.VMEM((2, R, D), F32)],
        compiler_params=PARAMS,
        cost_estimate=pl.CostEstimate(flops=9 * 10 ** 9, bytes_accessed=0, transcendentals=0),
        name="first_scores",
    )(qg[0], qg[1], *kv)


def last_scores_body(second, third, ks, p_in, st_in, p_ref, st_ref, st):
    st_ref[...] = st_in[...]
    for n, q in ((2, second), (3, third)):
        for h in range(2):
            score_chunk(n, h, q, ks[h], p_ref, st.at[n - 2])
        st_ref[:, chunk(n)] = st[n - 2].T[0:8, :]


def last_scores(qg, ks, p, st):
    return pl.pallas_call(
        last_scores_body,
        in_specs=[VM] * 5,
        out_specs=[VM] * 2,
        out_shape=[pltpu.VMEM((2, NQ, NK), BF), pltpu.VMEM((8, NQ), F32)],
        scratch_shapes=[pltpu.VMEM((2, R, D), F32)],
        input_output_aliases={3: 0},
        compiler_params=PARAMS,
        cost_estimate=pl.CostEstimate(flops=3 * 10 ** 9, bytes_accessed=0, transcendentals=0),
        name="last_scores",
    )(qg[2], qg[3], ks, p, st)


def merged(a, b, m):
    b = jnp.concatenate([b[0:4, chunk(n ^ m)] for n in range(4)], axis=1)
    top = jnp.maximum(a[0:2], b[0:2])
    total = a[2:4] * jnp.exp2(a[0:2] - top) + b[2:4] * jnp.exp2(b[0:2] - top)
    return top, total


def merge_body(a, b, after, out):
    top, total = merged(a[...], b[...], 1)
    out[0:2] = top
    out[2:4] = total
    out[4:8] = jnp.zeros((4, NQ), F32)


def merge(a, b, after):
    return pl.pallas_call(
        merge_body,
        in_specs=[VM] * 3,
        out_specs=VM,
        out_shape=pltpu.VMEM((8, NQ), F32),
        compiler_params=PARAMS,
        name="merge",
    )(a, b, after)


def score_grads_body(h, *refs):
    qg, kv, ks, p_ref = refs[0:4], refs[4:8], refs[8], refs[9]
    ds_ref, dq_ref, vs, gs = refs[10:]
    row = lax.broadcasted_iota(jnp.int32, (16, NK), 0)
    for n in range(4):
        vs[0:D, chunk(n)] = kv[n][head(h, 256), :]
        gs[n, 0:D, :] = qg[n][head(h, 256), :]
        gs[n, D:D + 16, :] = qg[n][512:528, :]
    vs[D:D + 16, :] = jnp.where((row >= 3 * h) & (row < 3 * h + 3), -1.0, 0.0).astype(BF)
    for n in range(4):
        pg = dot(gs[n], vs[...], 0, 0)
        ds = (p_ref[h, chunk(n), :].astype(F32) * pg).astype(BF)
        ds_ref[chunk(n), :] = ds
        dq_ref[chunk(n), :] = dot(ds, ks[h, 0:D], 1, 1)


def score_grads(h, qg, kv, ks, p):
    return pl.pallas_call(
        lambda *refs: score_grads_body(h, *refs),
        in_specs=[VM] * 10,
        out_specs=[VM] * 2,
        out_shape=[pltpu.VMEM((NQ, NK), BF), pltpu.VMEM((NQ, D), F32)],
        scratch_shapes=[
            pltpu.VMEM((D + 16, NK), BF),
            pltpu.VMEM((4, D + 16, R), BF),
        ],
        compiler_params=PARAMS,
        name="score_grads",
    )(*qg, *kv, ks, p)


def key_part(out, xs, ds, p_ref, cols):
    for h in range(2):
        out[head(h), :] = dot(xs[h, 0], ds[h][:, cols], 1, 0).astype(out.dtype)
        out[head(h, 256), :] = dot(xs[h, 1], p_ref[h, :, cols], 1, 0).astype(out.dtype)


def prior_partner_body(*refs):
    qg, own, pair, other, p_ref, ds, dqs = refs[0:4], *refs[4:8], refs[8:10], refs[10:12]
    out, xs, near, far = refs[12:]
    top, total = merged(pair[...], other[...], 2)
    f = jnp.exp2(own[0:2] - top) / total
    cols = jnp.concatenate([f * SCALE, jnp.zeros((6, NQ), F32)], axis=0).T
    for place, n in ((0, 0), (1, 1)):
        for h, dq in enumerate(dqs):
            near[chunk(place), head(h)] = dq[chunk(n), :] * cols[chunk(n), h:h + 1]
    for place, n in ((0, 2), (1, 3)):
        for h, dq in enumerate(dqs):
            far[chunk(place), head(h)] = (dq[chunk(n), :] * cols[chunk(n), h:h + 1]).astype(BF)
    for h in range(2):
        for n in range(4):
            fn = f[h:h + 1, chunk(n)]
            xs[h, 0, :, chunk(n)] = (qg[n][head(h), :].astype(F32) * (fn * SCALE)).astype(BF)
            xs[h, 1, :, chunk(n)] = (qg[n][head(h, 256), :].astype(F32) * fn).astype(BF)
    key_part(out, xs, ds, p_ref, chunk(3))


def prior_partner(qg, own, pair, other, p, ds, dq):
    return pl.pallas_call(
        prior_partner_body,
        in_specs=[VM] * 12,
        out_specs=[VM] * 4,
        out_shape=[
            pltpu.VMEM((512, R), BF),
            pltpu.VMEM((2, 2, D, NQ), BF),
            pltpu.VMEM((2 * R, 2 * D), F32),
            pltpu.VMEM((2 * R, 2 * D), BF),
        ],
        compiler_params=PARAMS,
        name="prior_partner",
    )(*qg, own, pair, other, p, *ds, *dq)


def key_grads_body(xs, p_ref, ds0, ds1, own_partner, prior, own):
    ds = (ds0, ds1)
    key_part(own_partner, xs, ds, p_ref, chunk(1))
    key_part(prior, xs, ds, p_ref, chunk(2))
    key_part(own, xs, ds, p_ref, chunk(0))


def key_grads(xs, p, ds):
    part = pltpu.VMEM((512, R), F32)
    return pl.pallas_call(
        key_grads_body,
        in_specs=[VM] * 4,
        out_specs=[VM] * 3,
        out_shape=[pltpu.VMEM((512, R), BF), part, part],
        compiler_params=PARAMS,
        name="key_grads",
    )(xs, p, *ds)


def prior_sum_body(a, b, after, out):
    out[...] = (a[...] + b[...].astype(F32)).astype(BF)


def prior_sum(a, b, after):
    return pl.pallas_call(
        prior_sum_body,
        in_specs=[VM] * 3,
        out_specs=VM,
        out_shape=pltpu.VMEM((512, R), BF),
        compiler_params=PARAMS,
        name="prior_sum",
    )(a, b, after)


def query_mid_body(near, far, after, own, pair):
    own[...] = near[chunk(0), :] + far[chunk(0), :].astype(F32)
    pair[...] = (near[chunk(1), :] + far[chunk(1), :].astype(F32)).astype(BF)


def query_mid(near, far, after):
    return pl.pallas_call(
        query_mid_body,
        in_specs=[VM] * 3,
        out_specs=[VM] * 2,
        out_shape=[pltpu.VMEM((R, 2 * D), F32), pltpu.VMEM((R, 2 * D), BF)],
        compiler_params=PARAMS,
        name="query_mid",
    )(near, far, after)


def query_sum_body(own, pair, out):
    out[...] = (own[...] + pair[...].astype(F32)).astype(BF)


def query_sum(own, pair):
    return pl.pallas_call(
        query_sum_body,
        in_specs=[VM] * 2,
        out_shape=jax.ShapeDtypeStruct((R, 2 * D), BF),
        compiler_params=PARAMS,
        cost_estimate=pl.CostEstimate(flops=6 * 10 ** 9, bytes_accessed=0, transcendentals=0),
        name="query_sum",
    )(own, pair)


def own_sum_body(own, other, out):
    out[...] = own[...] + other[...].astype(F32)


def own_sum(own, other):
    return pl.pallas_call(
        own_sum_body,
        in_specs=[VM] * 2,
        out_specs=VM,
        out_shape=pltpu.VMEM((512, R), F32),
        compiler_params=PARAMS,
        cost_estimate=pl.CostEstimate(flops=8 * 10 ** 9, bytes_accessed=0, transcendentals=0),
        name="own_sum",
    )(own, other)


def key_sum_body(own, back, dk, dv):
    total = own[...] + back[...].astype(F32)
    dk[...] = total[0:256].T.astype(BF)
    dv[...] = total[256:512].T.astype(BF)


def key_sum(own, back):
    return pl.pallas_call(
        key_sum_body,
        in_specs=[VM] * 2,
        out_shape=[jax.ShapeDtypeStruct((R, 2 * D), BF)] * 2,
        compiler_params=PARAMS,
        name="key_sum",
    )(own, back)


def along_y(value, turn):
    outer, inner = lax.axis_size("outer"), lax.axis_size("inner")
    pairs = [
        (o * inner + i, o * inner + (i ^ (6 if o % 2 == turn else 2))) for o in range(outer) for i in range(inner)
    ]
    return lax.ppermute(value, ("outer", "inner"), pairs)


def along_x(value):
    return lax.ppermute(value, "inner", [(i, i ^ 1) for i in range(8)])


def window_pairs():
    outer, inner = lax.axis_size("outer"), lax.axis_size("inner")
    turn = outer // 2
    return [
        (o * inner + i, (o + 1) % outer * inner + (i ^ 1 if o % turn == turn - 1 else i))
        for o in range(outer)
        for i in range(inner)
    ]


def to_next(value):
    return lax.ppermute(value, ("outer", "inner"), window_pairs())


def to_prior(value):
    return lax.ppermute(value, ("outer", "inner"), [(b, a) for a, b in window_pairs()])


def on_device(queries, key_rows, value_rows, outputs, out_grad):
    kv_own = pack_keys(key_rows, value_rows)
    qg_own = pack_queries(queries, outputs, out_grad)
    kv_prior = to_next(kv_own)
    kv_partner = along_x(kv_own)
    kv = [kv_own, kv_partner, kv_prior, to_next(kv_partner)]
    qg_first = along_y(qg_own, 0)
    qg = [qg_own, qg_first, along_y(qg_own, 1), along_y(qg_first, 1)]
    p, st, ks = first_scores(qg, kv)
    p, st = last_scores(qg, ks, p, st)
    st_pair = along_y(st, 0)
    ds0, dq0 = score_grads(0, qg, kv, ks, p)
    pair = merge(st, st_pair, dq0)
    pair_other = along_y(pair, 1)
    ds1, dq1 = score_grads(1, qg, kv, ks, p)
    ds, dq = (ds0, ds1), (dq0, dq1)
    part, xs, near, far = prior_partner(qg, st, pair, pair_other, p, ds, dq)
    part = along_x(part)
    far = along_y(far, 1)
    own_partner, prior, own = key_grads(xs, p, ds)
    other = along_x(own_partner)
    near, pair = query_mid(near, far, own_partner)
    query_grad = query_sum(near, along_y(pair, 0))
    back = to_prior(prior_sum(prior, part, pair))
    key_grad, value_grad = key_sum(own_sum(own, other), back)
    return query_grad, key_grad, value_grad


def solution(mesh):
    spec = P(("outer", "inner"), None)
    return jax.shard_map(
        on_device, mesh=mesh, in_specs=(spec,) * 5, out_specs=(spec,) * 3, check_vma=False
    )
```

```python
import jax
import jax.numpy as jnp
from jax import lax
from jax.experimental import pallas as pl
from jax.experimental.pallas import tpu as pltpu
from jax.sharding import PartitionSpec as P

R = 384
D = 128
SCALE = D ** -0.5
C = SCALE * 1.4426950408889634
NQ = 4 * R
NK = 4 * R
GROUPS = (slice(0, 3 * R), slice(3 * R, NK))
F32 = jnp.float32
BF = jnp.bfloat16
VM = pl.BlockSpec(memory_space=pltpu.VMEM)
HBM = pl.BlockSpec(memory_space=pltpu.HBM)
PARAMS = pltpu.CompilerParams(vmem_limit_bytes=16 * 1024 * 1024)
ALONE = pltpu.CompilerParams(vmem_limit_bytes=60 * 1024 * 1024)


def dot(a, b, ca, cb):
    return lax.dot_general(a, b, (((ca,), (cb,)), ((), ())), preferred_element_type=F32)


def chunk(n):
    return slice(n * R, (n + 1) * R)


def head(h, base=0):
    return slice(base + h * D, base + (h + 1) * D)


def turned(ref):
    return ref[...].astype(F32).T


def pack_keys_body(k, v, q, o, g, kv, qs, os, gs, ks, vs, sems):
    copies = [
        pltpu.make_async_copy(src, dst, sems.at[n])
        for n, (src, dst) in enumerate(((k, ks), (v, vs), (q, qs), (o, os), (g, gs)))
    ]
    for copy in copies:
        copy.start()
    copies[0].wait()
    kv[0:256] = turned(ks).astype(BF)
    copies[1].wait()
    kv[256:512] = turned(vs).astype(BF)
    for copy in copies[2:]:
        copy.wait()


def pack_keys(k, v, q, o, g):
    return pl.pallas_call(
        pack_keys_body,
        in_specs=[HBM] * 5,
        out_specs=[VM] * 4,
        out_shape=[pltpu.VMEM((512, R), BF)] + [pltpu.VMEM((R, 2 * D), BF)] * 3,
        scratch_shapes=[pltpu.VMEM((R, 2 * D), BF)] * 2 + [pltpu.SemaphoreType.DMA((5,))],
        compiler_params=ALONE,
        name="pack_keys",
    )(k, v, q, o, g)


def pack_queries_body(q, o, g, qg):
    qg[0:256] = turned(q).astype(BF)
    grads = turned(g)
    qg[256:512] = grads.astype(BF)
    prod = grads * turned(o)
    rows = []
    for h in range(2):
        d = jnp.sum(prod[head(h)], axis=0, keepdims=True)
        hi = d.astype(BF).astype(F32)
        mid = (d - hi).astype(BF).astype(F32)
        rows += [hi, mid, d - hi - mid]
    qg[512:528] = jnp.concatenate(rows + [jnp.zeros((10, R), F32)], axis=0).astype(BF)


def pack_queries(q, o, g):
    return pl.pallas_call(
        pack_queries_body,
        in_specs=[VM] * 3,
        out_specs=VM,
        out_shape=pltpu.VMEM((528, R), BF),
        compiler_params=PARAMS,
        name="pack_queries",
    )(q, o, g)


def score_tile(n, h, q, ks, group, cols, p_ref, st):
    scaled = q[head(h), :].astype(F32) * C
    high = scaled.astype(BF)
    low = (scaled - high.astype(F32)).astype(BF)
    s = dot(jnp.concatenate([high, low], axis=0), ks[h, :, cols], 0, 0)
    m = jnp.max(s, axis=1, keepdims=True)
    p = jnp.exp2(s - m)
    at = 4 * group + h
    st[n, :, at:at + 1] = m
    st[n, :, at + 2:at + 3] = jnp.sum(p, axis=1, keepdims=True)
    p_ref[h, chunk(n), cols] = p.astype(BF)
    return m


def lay_keys(ks, n, ref):
    for h in range(2):
        ks[h, 0:D, chunk(n)] = ref[head(h), :]
        ks[h, D:2 * D, chunk(n)] = ref[head(h), :]


def first_scores_body(own, first, second, k0, k1, k2, p_ref, st_ref, ks, st):
    for n, ref in enumerate((k0, k1, k2)):
        lay_keys(ks, n, ref)
    for n, q in enumerate((own, first, second)):
        for h in range(2):
            score_tile(n, h, q, ks, 0, GROUPS[0], p_ref, st)
        st_ref[0:4, chunk(n)] = st[n].T[0:4, :]


def first_scores(qg, kv):
    return pl.pallas_call(
        first_scores_body,
        in_specs=[VM] * 6,
        out_specs=[VM] * 3,
        out_shape=[pltpu.VMEM((2, NQ, NK), BF), pltpu.VMEM((8, NQ), F32), pltpu.VMEM((2, 2 * D, NK), BF)],
        scratch_shapes=[pltpu.VMEM((3, R, D), F32)],
        compiler_params=PARAMS,
        cost_estimate=pl.CostEstimate(flops=3 * 10 ** 9, bytes_accessed=0, transcendentals=0),
        name="first_scores",
    )(*qg[0:3], *kv[0:3])


def last_keys_body(k3, ks_in, ks):
    lay_keys(ks, 3, k3)


def last_keys(k3, ks):
    return pl.pallas_call(
        last_keys_body,
        in_specs=[VM] * 2,
        out_specs=VM,
        out_shape=pltpu.VMEM((2, 2 * D, NK), BF),
        input_output_aliases={1: 0},
        compiler_params=PARAMS,
        cost_estimate=pl.CostEstimate(flops=6 * 10 ** 9, bytes_accessed=0, transcendentals=0),
        name="last_keys",
    )(k3, ks)


def last_scores_body(own, first, second, third, ks, p_in, st_in, p_ref, st_ref, both_ref, st):
    st_ref[0:4, 0:3 * R] = st_in[0:4, 0:3 * R]
    for n, q in enumerate((own, first, second, third)):
        for h in range(2):
            if n == 3:
                m = score_tile(n, h, q, ks, 0, slice(0, NK), p_ref, st)
                st[n, :, 4 + h:5 + h] = m
                st[n, :, 6 + h:7 + h] = jnp.zeros((R, 1), F32)
            else:
                score_tile(n, h, q, ks, 1, GROUPS[1], p_ref, st)
        rows = st[n].T
        if n == 3:
            st_ref[0:4, chunk(n)] = rows[0:4, :]
        st_ref[4:8, chunk(n)] = rows[4:8, :]
    top, total = combined(st_ref[0:2], st_ref[2:4], st_ref[4:6], st_ref[6:8])
    both_ref[0:2] = top
    both_ref[2:4] = total
    both_ref[4:8] = jnp.zeros((4, NQ), F32)


def last_scores(qg, ks, p, st):
    return pl.pallas_call(
        last_scores_body,
        in_specs=[VM] * 7,
        out_specs=[VM] * 3,
        out_shape=[pltpu.VMEM((2, NQ, NK), BF), pltpu.VMEM((8, NQ), F32), pltpu.VMEM((8, NQ), F32)],
        scratch_shapes=[pltpu.VMEM((4, R, D), F32)],
        input_output_aliases={5: 0},
        compiler_params=PARAMS,
        cost_estimate=pl.CostEstimate(flops=2 * 10 ** 9, bytes_accessed=0, transcendentals=0),
        name="last_scores",
    )(*qg, ks, p, st)


def combined(m0, l0, m1, l1):
    top = jnp.maximum(m0, m1)
    return top, l0 * jnp.exp2(m0 - top) + l1 * jnp.exp2(m1 - top)


def merged(a, b, m):
    b = jnp.concatenate([b[0:4, chunk(n ^ m)] for n in range(4)], axis=1)
    return combined(a[0:2], a[2:4], b[0:2], b[2:4])


def merge_body(a, b, after, out):
    top, total = merged(a[...], b[...], 1)
    out[0:2] = top
    out[2:4] = total
    out[4:8] = jnp.zeros((4, NQ), F32)


def merge(a, b, after):
    return pl.pallas_call(
        merge_body,
        in_specs=[VM] * 3,
        out_specs=VM,
        out_shape=pltpu.VMEM((8, NQ), F32),
        compiler_params=PARAMS,
        name="merge",
    )(a, b, after)


def score_grads_body(h, *refs):
    qg, kv, ks, p_ref = refs[0:4], refs[4:8], refs[8], refs[9]
    ds_ref, dq_ref, vs, gs = refs[10:]
    row = lax.broadcasted_iota(jnp.int32, (16, NK), 0)
    for n in range(4):
        vs[0:D, chunk(n)] = kv[n][head(h, 256), :]
        gs[n, 0:D, :] = qg[n][head(h, 256), :]
        gs[n, D:D + 16, :] = qg[n][512:528, :]
    vs[D:D + 16, :] = jnp.where((row >= 3 * h) & (row < 3 * h + 3), -1.0, 0.0).astype(BF)
    for n in range(4):
        pg = dot(gs[n], vs[...], 0, 0)
        ds = (p_ref[h, chunk(n), :].astype(F32) * pg).astype(BF)
        ds_ref[chunk(n), :] = ds
        for group, cols in enumerate(GROUPS):
            dq_ref[group, chunk(n), :] = dot(ds[:, cols], ks[h, 0:D, cols], 1, 1)


def score_grads(h, qg, kv, ks, p):
    return pl.pallas_call(
        lambda *refs: score_grads_body(h, *refs),
        in_specs=[VM] * 10,
        out_specs=[VM] * 2,
        out_shape=[pltpu.VMEM((NQ, NK), BF), pltpu.VMEM((2, NQ, D), F32)],
        scratch_shapes=[
            pltpu.VMEM((D + 16, NK), BF),
            pltpu.VMEM((4, D + 16, R), BF),
        ],
        compiler_params=PARAMS,
        name="score_grads",
    )(*qg, *kv, ks, p)


def key_part(out, xs, ds, p_ref, cols):
    for h in range(2):
        out[head(h), :] = dot(xs[h, 0], ds[h][:, cols], 1, 0).astype(out.dtype)
        out[head(h, 256), :] = dot(xs[h, 1], p_ref[h, :, cols], 1, 0).astype(out.dtype)


def scaled_rows(xs, qg, f):
    for h in range(2):
        for n in range(4):
            fn = f[h:h + 1, chunk(n)]
            xs[h, 0, :, chunk(n)] = (qg[n][head(h), :].astype(F32) * (fn * SCALE)).astype(BF)
            xs[h, 1, :, chunk(n)] = (qg[n][head(h, 256), :].astype(F32) * fn).astype(BF)


def prior_partner_body(*refs):
    qg, st, pair, other, p_ref, ds, dqs = refs[0:4], *refs[4:8], refs[8:10], refs[10:12]
    out, f_ref, near, far, xs = refs[12:]
    top, total = merged(pair[...], other[...], 2)
    f = [jnp.exp2(st[4 * group:4 * group + 2] - top) / total for group in range(2)]
    f_ref[0:2] = f[0]
    f_ref[2:8] = jnp.zeros((6, NQ), F32)
    scaled_rows(xs, qg, f[1])
    key_part(out, xs, ds, p_ref, chunk(3))
    out[512:528] = jnp.zeros((16, R), BF)
    cols = (jnp.concatenate([*f, jnp.zeros((4, NQ), F32)], axis=0) * SCALE).T
    for n in range(4):
        rows = chunk(n)
        for h, dq in enumerate(dqs):
            total = dq[0, rows] * cols[rows, h:h + 1] + dq[1, rows] * cols[rows, 2 + h:3 + h]
            if n < 2:
                near[chunk(n), head(h)] = total
            else:
                far[chunk(n - 2), head(h)] = total.astype(BF)


def prior_partner(qg, st, pair, other, p, ds, dq):
    return pl.pallas_call(
        prior_partner_body,
        in_specs=[VM] * 12,
        out_specs=[VM] * 4,
        out_shape=[
            pltpu.VMEM((528, R), BF),
            pltpu.VMEM((8, NQ), F32),
            pltpu.VMEM((2 * R, 2 * D), F32),
            pltpu.VMEM((2 * R, 2 * D), BF),
        ],
        scratch_shapes=[pltpu.VMEM((2, 2, D, NQ), BF)],
        compiler_params=PARAMS,
        name="prior_partner",
    )(*qg, st, pair, other, p, *ds, *dq)


def key_grads_body(*refs):
    qg, f_ref, p_ref, ds = refs[0:4], refs[4], refs[5], refs[6:8]
    own_partner, prior, own, xs = refs[8:]
    scaled_rows(xs, qg, f_ref[0:2])
    key_part(own_partner, xs, ds, p_ref, chunk(1))
    key_part(prior, xs, ds, p_ref, chunk(2))
    key_part(own, xs, ds, p_ref, chunk(0))


def key_grads(qg, f, p, ds):
    part = pltpu.VMEM((512, R), F32)
    return pl.pallas_call(
        key_grads_body,
        in_specs=[VM] * 8,
        out_specs=[VM] * 3,
        out_shape=[pltpu.VMEM((512, R), BF), part, part],
        scratch_shapes=[pltpu.VMEM((2, 2, D, NQ), BF)],
        compiler_params=PARAMS,
        name="key_grads",
    )(*qg, f, p, *ds)


def middle_sums_body(prior, part, near, far, out, own, pair):
    out[...] = (prior[...] + part[0:512].astype(F32)).astype(BF)
    own[...] = near[chunk(0), :] + far[chunk(0), :].astype(F32)
    pair[...] = (near[chunk(1), :] + far[chunk(1), :].astype(F32)).astype(BF)


def middle_sums(prior, part, near, far):
    return pl.pallas_call(
        middle_sums_body,
        in_specs=[VM] * 4,
        out_specs=[VM] * 3,
        out_shape=[pltpu.VMEM((512, R), BF), pltpu.VMEM((R, 2 * D), F32), pltpu.VMEM((R, 2 * D), BF)],
        compiler_params=PARAMS,
        name="middle_sums",
    )(prior, part, near, far)


def query_sum_body(own, pair, out):
    out[...] = (own[...] + pair[...].astype(F32)).astype(BF)


def query_sum(own, pair):
    return pl.pallas_call(
        query_sum_body,
        in_specs=[VM] * 2,
        out_shape=jax.ShapeDtypeStruct((R, 2 * D), BF),
        compiler_params=PARAMS,
        cost_estimate=pl.CostEstimate(flops=2 * 10 ** 9, bytes_accessed=0, transcendentals=0),
        name="query_sum",
    )(own, pair)


def own_sum_body(own, other, out):
    out[...] = own[...] + other[...].astype(F32)


def own_sum(own, other):
    return pl.pallas_call(
        own_sum_body,
        in_specs=[VM] * 2,
        out_specs=VM,
        out_shape=pltpu.VMEM((512, R), F32),
        compiler_params=PARAMS,
        cost_estimate=pl.CostEstimate(flops=8 * 10 ** 9, bytes_accessed=0, transcendentals=0),
        name="own_sum",
    )(own, other)


def key_sum_body(own, back, dk, dv):
    total = own[...] + back[...].astype(F32)
    dk[...] = total[0:256].T.astype(BF)
    dv[...] = total[256:512].T.astype(BF)


def key_sum(own, back):
    return pl.pallas_call(
        key_sum_body,
        in_specs=[VM] * 2,
        out_shape=[jax.ShapeDtypeStruct((R, 2 * D), BF)] * 2,
        compiler_params=PARAMS,
        name="key_sum",
    )(own, back)


def along_y(value, turn):
    outer, inner = lax.axis_size("outer"), lax.axis_size("inner")
    pairs = [
        (o * inner + i, o * inner + (i ^ (6 if o % 2 == turn else 2))) for o in range(outer) for i in range(inner)
    ]
    return lax.ppermute(value, ("outer", "inner"), pairs)


def along_x(value):
    return lax.ppermute(value, "inner", [(i, i ^ 1) for i in range(8)])


def window_pairs():
    outer, inner = lax.axis_size("outer"), lax.axis_size("inner")
    turn = outer // 2
    return [
        (o * inner + i, (o + 1) % outer * inner + (i ^ 1 if o % turn == turn - 1 else i))
        for o in range(outer)
        for i in range(inner)
    ]


def to_next(value):
    return lax.ppermute(value, ("outer", "inner"), window_pairs())


def to_prior(value):
    return lax.ppermute(value, ("outer", "inner"), [(b, a) for a, b in window_pairs()])


def on_device(queries, key_rows, value_rows, outputs, out_grad):
    kv_own, *rest = pack_keys(key_rows, value_rows, queries, outputs, out_grad)
    qg_own = pack_queries(*rest)
    kv_prior = to_next(kv_own)
    kv_partner = along_x(kv_own)
    kv = [kv_own, kv_partner, kv_prior, to_next(kv_partner)]
    qg_first = along_y(qg_own, 0)
    qg = [qg_own, qg_first, along_y(qg_own, 1), along_y(qg_first, 1)]
    p, st, ks = first_scores(qg, kv)
    ks = last_keys(kv[3], ks)
    p, st, both = last_scores(qg, ks, p, st)
    both_pair = along_y(both, 0)
    ds0, dq0 = score_grads(0, qg, kv, ks, p)
    pair = merge(both, both_pair, dq0)
    pair_other = along_y(pair, 1)
    ds1, dq1 = score_grads(1, qg, kv, ks, p)
    ds, dq = (ds0, ds1), (dq0, dq1)
    part, f, near, far = prior_partner(qg, st, pair, pair_other, p, ds, dq)
    part = along_x(part)
    far = along_y(far, 1)
    own_partner, prior, own = key_grads(qg, f, p, ds)
    other = along_x(own_partner)
    prior, near, pair = middle_sums(prior, part, near, far)
    back = to_prior(prior)
    query_grad = query_sum(near, along_y(pair, 0))
    key_grad, value_grad = key_sum(own_sum(own, other), back)
    return query_grad, key_grad, value_grad


def solution(mesh):
    spec = P(("outer", "inner"), None)
    return jax.shard_map(
        on_device, mesh=mesh, in_specs=(spec,) * 5, out_specs=(spec,) * 3, check_vma=False
    )
```

```python
import jax
import jax.numpy as jnp
from jax import lax
from jax.experimental import pallas as pl
from jax.experimental.pallas import tpu as pltpu
from jax.sharding import PartitionSpec as P

R = 384
D = 128
SCALE = D ** -0.5
C = SCALE * 1.4426950408889634
NQ = 4 * R
NK = 4 * R
GROUPS = (slice(0, 3 * R), slice(3 * R, NK))
F32 = jnp.float32
BF = jnp.bfloat16
VM = pl.BlockSpec(memory_space=pltpu.VMEM)
HBM = pl.BlockSpec(memory_space=pltpu.HBM)
PARAMS = pltpu.CompilerParams(vmem_limit_bytes=16 * 1024 * 1024)
ALONE = pltpu.CompilerParams(vmem_limit_bytes=60 * 1024 * 1024)


def dot(a, b, ca, cb):
    return lax.dot_general(a, b, (((ca,), (cb,)), ((), ())), preferred_element_type=F32)


def chunk(n):
    return slice(n * R, (n + 1) * R)


def head(h, base=0):
    return slice(base + h * D, base + (h + 1) * D)


def turned(ref):
    return ref[...].astype(F32).T


def pack_keys_body(k, v, q, o, g, kv, padded, qs, os, gs, ks, vs, sems):
    copies = [
        pltpu.make_async_copy(src, dst, sems.at[n])
        for n, (src, dst) in enumerate(((k, ks), (v, vs), (q, qs), (o, os), (g, gs)))
    ]
    for copy in copies:
        copy.start()
    copies[0].wait()
    kv[0:256] = turned(ks).astype(BF)
    copies[1].wait()
    kv[256:512] = turned(vs).astype(BF)
    padded[0:512] = kv[...]
    padded[512:544] = jnp.zeros((32, R), BF)
    for copy in copies[2:]:
        copy.wait()


def pack_keys(k, v, q, o, g):
    return pl.pallas_call(
        pack_keys_body,
        in_specs=[HBM] * 5,
        out_specs=[VM] * 5,
        out_shape=[pltpu.VMEM((512, R), BF), pltpu.VMEM((544, R), BF)] + [pltpu.VMEM((R, 2 * D), BF)] * 3,
        scratch_shapes=[pltpu.VMEM((R, 2 * D), BF)] * 2 + [pltpu.SemaphoreType.DMA((5,))],
        compiler_params=ALONE,
        name="pack_keys",
    )(k, v, q, o, g)


def pack_queries_body(q, o, g, qg):
    qg[0:256] = turned(q).astype(BF)
    grads = turned(g)
    qg[256:512] = grads.astype(BF)
    prod = grads * turned(o)
    rows = []
    for h in range(2):
        d = jnp.sum(prod[head(h)], axis=0, keepdims=True)
        hi = d.astype(BF).astype(F32)
        mid = (d - hi).astype(BF).astype(F32)
        rows += [hi, mid, d - hi - mid]
    qg[512:528] = jnp.concatenate(rows + [jnp.zeros((10, R), F32)], axis=0).astype(BF)


def pack_queries(q, o, g):
    return pl.pallas_call(
        pack_queries_body,
        in_specs=[VM] * 3,
        out_specs=VM,
        out_shape=pltpu.VMEM((528, R), BF),
        compiler_params=PARAMS,
        name="pack_queries",
    )(q, o, g)


def score_tile(n, h, q, ks, group, cols, p_ref, st):
    scaled = q[head(h), :].astype(F32) * C
    high = scaled.astype(BF)
    low = (scaled - high.astype(F32)).astype(BF)
    s = dot(jnp.concatenate([high, low], axis=0), ks[h, :, cols], 0, 0)
    m = jnp.max(s, axis=1, keepdims=True)
    p = jnp.exp2(s - m)
    at = 4 * group + h
    st[n, :, at:at + 1] = m
    st[n, :, at + 2:at + 3] = jnp.sum(p, axis=1, keepdims=True)
    p_ref[h, chunk(n), cols] = p.astype(BF)
    return m


def lay_keys(ks, n, ref):
    for h in range(2):
        ks[h, 0:D, chunk(n)] = ref[head(h), :]
        ks[h, D:2 * D, chunk(n)] = ref[head(h), :]


def first_scores_body(own, first, second, k0, k1, k2, p_ref, st_ref, ks, st):
    for n, ref in enumerate((k0, k1, k2)):
        lay_keys(ks, n, ref)
    for n, q in enumerate((own, first, second)):
        for h in range(2):
            score_tile(n, h, q, ks, 0, GROUPS[0], p_ref, st)
        st_ref[0:4, chunk(n)] = st[n].T[0:4, :]


def first_scores(qg, kv):
    return pl.pallas_call(
        first_scores_body,
        in_specs=[VM] * 6,
        out_specs=[VM] * 3,
        out_shape=[pltpu.VMEM((2, NQ, NK), BF), pltpu.VMEM((8, NQ), F32), pltpu.VMEM((2, 2 * D, NK), BF)],
        scratch_shapes=[pltpu.VMEM((3, R, D), F32)],
        compiler_params=PARAMS,
        cost_estimate=pl.CostEstimate(flops=15 * 10 ** 8, bytes_accessed=0, transcendentals=0),
        name="first_scores",
    )(*qg[0:3], *kv[0:3])


def last_keys_body(k3, ks_in, ks):
    lay_keys(ks, 3, k3)


def last_keys(k3, ks):
    return pl.pallas_call(
        last_keys_body,
        in_specs=[VM] * 2,
        out_specs=VM,
        out_shape=pltpu.VMEM((2, 2 * D, NK), BF),
        input_output_aliases={1: 0},
        compiler_params=PARAMS,
        cost_estimate=pl.CostEstimate(flops=10 * 10 ** 8, bytes_accessed=0, transcendentals=0),
        name="last_keys",
    )(k3, ks)


def last_scores_body(own, first, second, third, ks, p_in, st_in, p_ref, st_ref, both_ref, st):
    st_ref[0:4, 0:3 * R] = st_in[0:4, 0:3 * R]
    for n, q in enumerate((own, first, second, third)):
        for h in range(2):
            if n == 3:
                m = score_tile(n, h, q, ks, 0, slice(0, NK), p_ref, st)
                st[n, :, 4 + h:5 + h] = m
                st[n, :, 6 + h:7 + h] = jnp.zeros((R, 1), F32)
            else:
                score_tile(n, h, q, ks, 1, GROUPS[1], p_ref, st)
        rows = st[n].T
        if n == 3:
            st_ref[0:4, chunk(n)] = rows[0:4, :]
        st_ref[4:8, chunk(n)] = rows[4:8, :]
    top, total = combined(st_ref[0:2], st_ref[2:4], st_ref[4:6], st_ref[6:8])
    both_ref[0:2] = top
    both_ref[2:4] = total
    both_ref[4:8] = jnp.zeros((4, NQ), F32)


def last_scores(qg, ks, p, st):
    return pl.pallas_call(
        last_scores_body,
        in_specs=[VM] * 7,
        out_specs=[VM] * 3,
        out_shape=[pltpu.VMEM((2, NQ, NK), BF), pltpu.VMEM((8, NQ), F32), pltpu.VMEM((8, NQ), F32)],
        scratch_shapes=[pltpu.VMEM((4, R, D), F32)],
        input_output_aliases={5: 0},
        compiler_params=PARAMS,
        cost_estimate=pl.CostEstimate(flops=2 * 10 ** 9, bytes_accessed=0, transcendentals=0),
        name="last_scores",
    )(*qg, ks, p, st)


def combined(m0, l0, m1, l1):
    top = jnp.maximum(m0, m1)
    return top, l0 * jnp.exp2(m0 - top) + l1 * jnp.exp2(m1 - top)


def merged(a, b, m):
    b = jnp.concatenate([b[0:4, chunk(n ^ m)] for n in range(4)], axis=1)
    return combined(a[0:2], a[2:4], b[0:2], b[2:4])


def merge_body(a, b, after, out):
    top, total = merged(a[...], b[...], 1)
    out[0:2] = top
    out[2:4] = total
    out[4:8] = jnp.zeros((4, NQ), F32)


def merge(a, b, after):
    return pl.pallas_call(
        merge_body,
        in_specs=[VM] * 3,
        out_specs=VM,
        out_shape=pltpu.VMEM((8, NQ), F32),
        compiler_params=PARAMS,
        name="merge",
    )(a, b, after)


def score_grads_body(h, *refs):
    qg, kv, ks, p_ref = refs[0:4], refs[4:8], refs[8], refs[9]
    ds_ref, dq_ref, vs, gs = refs[10:]
    row = lax.broadcasted_iota(jnp.int32, (16, NK), 0)
    for n in range(4):
        vs[0:D, chunk(n)] = kv[n][head(h, 256), :]
        gs[n, 0:D, :] = qg[n][head(h, 256), :]
        gs[n, D:D + 16, :] = qg[n][512:528, :]
    vs[D:D + 16, :] = jnp.where((row >= 3 * h) & (row < 3 * h + 3), -1.0, 0.0).astype(BF)
    for n in range(4):
        pg = dot(gs[n], vs[...], 0, 0)
        ds = (p_ref[h, chunk(n), :].astype(F32) * pg).astype(BF)
        ds_ref[chunk(n), :] = ds
        for group, cols in enumerate(GROUPS):
            dq_ref[group, chunk(n), :] = dot(ds[:, cols], ks[h, 0:D, cols], 1, 1)


def score_grads(h, qg, kv, ks, p):
    return pl.pallas_call(
        lambda *refs: score_grads_body(h, *refs),
        in_specs=[VM] * 10,
        out_specs=[VM] * 2,
        out_shape=[pltpu.VMEM((NQ, NK), BF), pltpu.VMEM((2, NQ, D), F32)],
        scratch_shapes=[
            pltpu.VMEM((D + 16, NK), BF),
            pltpu.VMEM((4, D + 16, R), BF),
        ],
        compiler_params=PARAMS,
        name="score_grads",
    )(*qg, *kv, ks, p)


def key_part(out, xs, ds, p_ref, cols):
    for h in range(2):
        out[head(h), :] = dot(xs[h, 0], ds[h][:, cols], 1, 0).astype(out.dtype)
        out[head(h, 256), :] = dot(xs[h, 1], p_ref[h, :, cols], 1, 0).astype(out.dtype)


def scaled_rows(xs, qg, f):
    for h in range(2):
        for n in range(4):
            fn = f[h:h + 1, chunk(n)]
            xs[h, 0, :, chunk(n)] = (qg[n][head(h), :].astype(F32) * (fn * SCALE)).astype(BF)
            xs[h, 1, :, chunk(n)] = (qg[n][head(h, 256), :].astype(F32) * fn).astype(BF)


def prior_partner_body(*refs):
    qg, st, pair, other, p_ref, ds, dqs = refs[0:4], *refs[4:8], refs[8:10], refs[10:12]
    out, f_ref, near, far, xs = refs[12:]
    top, total = merged(pair[...], other[...], 2)
    f = [jnp.exp2(st[4 * group:4 * group + 2] - top) / total for group in range(2)]
    f_ref[0:2] = f[0]
    f_ref[2:8] = jnp.zeros((6, NQ), F32)
    scaled_rows(xs, qg, f[1])
    key_part(out, xs, ds, p_ref, chunk(3))
    out[512:528] = jnp.zeros((16, R), BF)
    cols = (jnp.concatenate([*f, jnp.zeros((4, NQ), F32)], axis=0) * SCALE).T
    for n in range(4):
        rows = chunk(n)
        for h, dq in enumerate(dqs):
            total = dq[0, rows] * cols[rows, h:h + 1] + dq[1, rows] * cols[rows, 2 + h:3 + h]
            if n < 2:
                near[chunk(n), head(h)] = total
            else:
                far[chunk(n - 2), head(h)] = total.astype(BF)


def prior_partner(qg, st, pair, other, p, ds, dq):
    return pl.pallas_call(
        prior_partner_body,
        in_specs=[VM] * 12,
        out_specs=[VM] * 4,
        out_shape=[
            pltpu.VMEM((528, R), BF),
            pltpu.VMEM((8, NQ), F32),
            pltpu.VMEM((2 * R, 2 * D), F32),
            pltpu.VMEM((2 * R, 2 * D), BF),
        ],
        scratch_shapes=[pltpu.VMEM((2, 2, D, NQ), BF)],
        compiler_params=PARAMS,
        name="prior_partner",
    )(*qg, st, pair, other, p, *ds, *dq)


def key_grads_body(*refs):
    qg, f_ref, p_ref, ds = refs[0:4], refs[4], refs[5], refs[6:8]
    own_partner, prior, own, xs = refs[8:]
    scaled_rows(xs, qg, f_ref[0:2])
    key_part(own_partner, xs, ds, p_ref, chunk(1))
    key_part(prior, xs, ds, p_ref, chunk(2))
    key_part(own, xs, ds, p_ref, chunk(0))


def key_grads(qg, f, p, ds):
    part = pltpu.VMEM((512, R), F32)
    return pl.pallas_call(
        key_grads_body,
        in_specs=[VM] * 8,
        out_specs=[VM] * 3,
        out_shape=[pltpu.VMEM((512, R), BF), part, part],
        scratch_shapes=[pltpu.VMEM((2, 2, D, NQ), BF)],
        compiler_params=PARAMS,
        name="key_grads",
    )(*qg, f, p, *ds)


def middle_sums_body(prior, part, near, far, out, own, pair):
    out[...] = (prior[...] + part[0:512].astype(F32)).astype(BF)
    own[...] = near[chunk(0), :] + far[chunk(0), :].astype(F32)
    pair[...] = (near[chunk(1), :] + far[chunk(1), :].astype(F32)).astype(BF)


def middle_sums(prior, part, near, far):
    return pl.pallas_call(
        middle_sums_body,
        in_specs=[VM] * 4,
        out_specs=[VM] * 3,
        out_shape=[pltpu.VMEM((512, R), BF), pltpu.VMEM((R, 2 * D), F32), pltpu.VMEM((R, 2 * D), BF)],
        compiler_params=PARAMS,
        name="middle_sums",
    )(prior, part, near, far)


def query_sum_body(own, pair, after, out):
    out[...] = (own[...] + pair[...].astype(F32)).astype(BF)


def query_sum(own, pair, after):
    return pl.pallas_call(
        query_sum_body,
        in_specs=[VM] * 3,
        out_shape=jax.ShapeDtypeStruct((R, 2 * D), BF),
        compiler_params=PARAMS,
        cost_estimate=pl.CostEstimate(flops=2 * 10 ** 9, bytes_accessed=0, transcendentals=0),
        name="query_sum",
    )(own, pair, after)


def own_sum_body(own, other, out):
    out[...] = own[...] + other[...].astype(F32)


def own_sum(own, other):
    return pl.pallas_call(
        own_sum_body,
        in_specs=[VM] * 2,
        out_specs=VM,
        out_shape=pltpu.VMEM((512, R), F32),
        compiler_params=PARAMS,
        cost_estimate=pl.CostEstimate(flops=8 * 10 ** 9, bytes_accessed=0, transcendentals=0),
        name="own_sum",
    )(own, other)


def key_sum_body(own, back, dk, dv, done):
    done[...] = jnp.zeros((8, D), F32)
    total = own[...] + back[...].astype(F32)
    dk[...] = total[0:256].T.astype(BF)
    dv[...] = total[256:512].T.astype(BF)


def key_sum(own, back):
    return pl.pallas_call(
        key_sum_body,
        in_specs=[VM] * 2,
        out_shape=[jax.ShapeDtypeStruct((R, 2 * D), BF)] * 2 + [pltpu.VMEM((8, D), F32)],
        compiler_params=PARAMS,
        name="key_sum",
    )(own, back)


def along_y(value, turn):
    outer, inner = lax.axis_size("outer"), lax.axis_size("inner")
    pairs = [
        (o * inner + i, o * inner + (i ^ (6 if o % 2 == turn else 2))) for o in range(outer) for i in range(inner)
    ]
    return lax.ppermute(value, ("outer", "inner"), pairs)


def along_x(value):
    return lax.ppermute(value, "inner", [(i, i ^ 1) for i in range(8)])


def window_pairs():
    outer, inner = lax.axis_size("outer"), lax.axis_size("inner")
    turn = outer // 2
    return [
        (o * inner + i, (o + 1) % outer * inner + (i ^ 1 if o % turn == turn - 1 else i))
        for o in range(outer)
        for i in range(inner)
    ]


def to_next(value):
    return lax.ppermute(value, ("outer", "inner"), window_pairs())


def to_prior(value):
    return lax.ppermute(value, ("outer", "inner"), [(b, a) for a, b in window_pairs()])


def on_device(queries, key_rows, value_rows, outputs, out_grad):
    kv_own, padded, *rest = pack_keys(key_rows, value_rows, queries, outputs, out_grad)
    qg_own = pack_queries(*rest)
    kv_prior = to_next(padded)
    kv_partner = along_x(kv_own)
    kv = [kv_own, kv_partner, kv_prior, to_next(kv_partner)]
    qg_first = along_y(qg_own, 0)
    qg = [qg_own, qg_first, along_y(qg_own, 1), along_y(qg_first, 1)]
    p, st, ks = first_scores(qg, kv)
    ks = last_keys(kv[3], ks)
    p, st, both = last_scores(qg, ks, p, st)
    both_pair = along_y(both, 0)
    ds0, dq0 = score_grads(0, qg, kv, ks, p)
    pair = merge(both, both_pair, dq0)
    pair_other = along_y(pair, 1)
    ds1, dq1 = score_grads(1, qg, kv, ks, p)
    ds, dq = (ds0, ds1), (dq0, dq1)
    part, f, near, far = prior_partner(qg, st, pair, pair_other, p, ds, dq)
    part = along_x(part)
    far = along_y(far, 1)
    own_partner, prior, own = key_grads(qg, f, p, ds)
    other = along_x(own_partner)
    prior, near, pair = middle_sums(prior, part, near, far)
    back = to_prior(prior)
    pair = along_y(pair, 0)
    key_grad, value_grad, done = key_sum(own_sum(own, other), back)
    query_grad = query_sum(near, pair, done)
    return query_grad, key_grad, value_grad


def solution(mesh):
    spec = P(("outer", "inner"), None)
    return jax.shard_map(
        on_device, mesh=mesh, in_specs=(spec,) * 5, out_specs=(spec,) * 3, check_vma=False
    )
```

```python
import jax
import jax.numpy as jnp
from jax import lax
from jax.experimental import pallas as pl
from jax.experimental.pallas import tpu as pltpu
from jax.sharding import PartitionSpec as P

R = 384
D = 128
SCALE = D ** -0.5
C = SCALE * 1.4426950408889634
NQ = 4 * R
NK = 4 * R
GROUPS = (slice(0, 3 * R), slice(3 * R, NK))
F32 = jnp.float32
BF = jnp.bfloat16
VM = pl.BlockSpec(memory_space=pltpu.VMEM)
HBM = pl.BlockSpec(memory_space=pltpu.HBM)
PARAMS = pltpu.CompilerParams(vmem_limit_bytes=16 * 1024 * 1024)
ALONE = pltpu.CompilerParams(vmem_limit_bytes=60 * 1024 * 1024)


def dot(a, b, ca, cb):
    return lax.dot_general(a, b, (((ca,), (cb,)), ((), ())), preferred_element_type=F32)


def chunk(n):
    return slice(n * R, (n + 1) * R)


def head(h, base=0):
    return slice(base + h * D, base + (h + 1) * D)


def turned(ref):
    return ref[...].astype(F32).T


def pack_keys_body(k, v, q, o, g, kv, padded, qs, os, gs, ks, vs, sems):
    copies = [
        pltpu.make_async_copy(src, dst, sems.at[n])
        for n, (src, dst) in enumerate(((k, ks), (v, vs), (q, qs), (o, os), (g, gs)))
    ]
    for copy in copies:
        copy.start()
    copies[0].wait()
    kv[0:256] = turned(ks).astype(BF)
    copies[1].wait()
    kv[256:512] = turned(vs).astype(BF)
    padded[0:512] = kv[...]
    padded[512:544] = jnp.zeros((32, R), BF)
    for copy in copies[2:]:
        copy.wait()


def pack_keys(k, v, q, o, g):
    return pl.pallas_call(
        pack_keys_body,
        in_specs=[HBM] * 5,
        out_specs=[VM] * 5,
        out_shape=[pltpu.VMEM((512, R), BF), pltpu.VMEM((544, R), BF)] + [pltpu.VMEM((R, 2 * D), BF)] * 3,
        scratch_shapes=[pltpu.VMEM((R, 2 * D), BF)] * 2 + [pltpu.SemaphoreType.DMA((5,))],
        compiler_params=ALONE,
        name="pack_keys",
    )(k, v, q, o, g)


def pack_queries_body(q, o, g, qg):
    qg[0:256] = turned(q).astype(BF)
    grads = turned(g)
    qg[256:512] = grads.astype(BF)
    prod = grads * turned(o)
    rows = []
    for h in range(2):
        d = jnp.sum(prod[head(h)], axis=0, keepdims=True)
        hi = d.astype(BF).astype(F32)
        mid = (d - hi).astype(BF).astype(F32)
        rows += [hi, mid, d - hi - mid]
    qg[512:528] = jnp.concatenate(rows + [jnp.zeros((10, R), F32)], axis=0).astype(BF)


def pack_queries(q, o, g):
    return pl.pallas_call(
        pack_queries_body,
        in_specs=[VM] * 3,
        out_specs=VM,
        out_shape=pltpu.VMEM((528, R), BF),
        compiler_params=PARAMS,
        name="pack_queries",
    )(q, o, g)


def score_tile(n, h, q, ks, group, cols, p_ref, st):
    scaled = q[head(h), :].astype(F32) * C
    high = scaled.astype(BF)
    low = (scaled - high.astype(F32)).astype(BF)
    s = dot(jnp.concatenate([high, low], axis=0), ks[h, :, cols], 0, 0)
    m = jnp.max(s, axis=1, keepdims=True)
    p = jnp.exp2(s - m)
    at = 4 * group + h
    st[n, :, at:at + 1] = m
    st[n, :, at + 2:at + 3] = jnp.sum(p, axis=1, keepdims=True)
    p_ref[h, chunk(n), cols] = p.astype(BF)
    return m


def lay_keys(ks, n, ref):
    for h in range(2):
        ks[h, 0:D, chunk(n)] = ref[head(h), :]
        ks[h, D:2 * D, chunk(n)] = ref[head(h), :]


def first_scores_body(own, first, second, k0, k1, k2, p_ref, st_ref, ks, st):
    for n, ref in enumerate((k0, k1, k2)):
        lay_keys(ks, n, ref)
    for n, q in enumerate((own, first, second)):
        for h in range(2):
            score_tile(n, h, q, ks, 0, GROUPS[0], p_ref, st)
        st_ref[0:4, chunk(n)] = st[n].T[0:4, :]


def first_scores(qg, kv):
    return pl.pallas_call(
        first_scores_body,
        in_specs=[VM] * 6,
        out_specs=[VM] * 3,
        out_shape=[pltpu.VMEM((2, NQ, NK), BF), pltpu.VMEM((8, NQ), F32), pltpu.VMEM((2, 2 * D, NK), BF)],
        scratch_shapes=[pltpu.VMEM((3, R, D), F32)],
        compiler_params=PARAMS,
        cost_estimate=pl.CostEstimate(flops=15 * 10 ** 8, bytes_accessed=0, transcendentals=0),
        name="first_scores",
    )(*qg[0:3], *kv[0:3])


def last_keys_body(k3, ks_in, ks):
    lay_keys(ks, 3, k3)


def last_keys(k3, ks):
    return pl.pallas_call(
        last_keys_body,
        in_specs=[VM] * 2,
        out_specs=VM,
        out_shape=pltpu.VMEM((2, 2 * D, NK), BF),
        input_output_aliases={1: 0},
        compiler_params=PARAMS,
        cost_estimate=pl.CostEstimate(flops=10 * 10 ** 8, bytes_accessed=0, transcendentals=0),
        name="last_keys",
    )(k3, ks)


def rest_scores_body(own, first, second, ks, p_in, st_in, p_ref, st_ref, st):
    st_ref[0:4, 0:3 * R] = st_in[0:4, 0:3 * R]
    st_ref[:, chunk(3)] = jnp.zeros((8, R), F32)
    for n, q in enumerate((own, first, second)):
        for h in range(2):
            score_tile(n, h, q, ks, 1, GROUPS[1], p_ref, st)
        st_ref[4:8, chunk(n)] = st[n].T[4:8, :]


def rest_scores(qg, ks, p, st):
    return pl.pallas_call(
        rest_scores_body,
        in_specs=[VM] * 6,
        out_specs=[VM] * 2,
        out_shape=[pltpu.VMEM((2, NQ, NK), BF), pltpu.VMEM((8, NQ), F32)],
        scratch_shapes=[pltpu.VMEM((3, R, D), F32)],
        input_output_aliases={4: 0},
        compiler_params=PARAMS,
        cost_estimate=pl.CostEstimate(flops=10 ** 9, bytes_accessed=0, transcendentals=0),
        name="rest_scores",
    )(*qg[0:3], ks, p, st)


def last_scores_body(third, ks, p_in, st_in, p_ref, st_ref, both_ref, st):
    st_ref[:, 0:3 * R] = st_in[:, 0:3 * R]
    for h in range(2):
        m = score_tile(3, h, third, ks, 0, slice(0, NK), p_ref, st)
        st[3, :, 4 + h:5 + h] = m
        st[3, :, 6 + h:7 + h] = jnp.zeros((R, 1), F32)
    st_ref[:, chunk(3)] = st[3].T[0:8, :]
    top, total = combined(st_ref[0:2], st_ref[2:4], st_ref[4:6], st_ref[6:8])
    both_ref[0:2] = top
    both_ref[2:4] = total
    both_ref[4:8] = jnp.zeros((4, NQ), F32)


def last_scores(third, ks, p, st):
    return pl.pallas_call(
        last_scores_body,
        in_specs=[VM] * 4,
        out_specs=[VM] * 3,
        out_shape=[pltpu.VMEM((2, NQ, NK), BF), pltpu.VMEM((8, NQ), F32), pltpu.VMEM((8, NQ), F32)],
        scratch_shapes=[pltpu.VMEM((4, R, D), F32)],
        input_output_aliases={2: 0},
        compiler_params=PARAMS,
        cost_estimate=pl.CostEstimate(flops=10 ** 9, bytes_accessed=0, transcendentals=0),
        name="last_scores",
    )(third, ks, p, st)


def combined(m0, l0, m1, l1):
    top = jnp.maximum(m0, m1)
    return top, l0 * jnp.exp2(m0 - top) + l1 * jnp.exp2(m1 - top)


def merged(a, b, m):
    b = jnp.concatenate([b[0:4, chunk(n ^ m)] for n in range(4)], axis=1)
    return combined(a[0:2], a[2:4], b[0:2], b[2:4])


def merge_body(a, b, after, out):
    top, total = merged(a[...], b[...], 1)
    out[0:2] = top
    out[2:4] = total
    out[4:8] = jnp.zeros((4, NQ), F32)


def merge(a, b, after):
    return pl.pallas_call(
        merge_body,
        in_specs=[VM] * 3,
        out_specs=VM,
        out_shape=pltpu.VMEM((8, NQ), F32),
        compiler_params=PARAMS,
        name="merge",
    )(a, b, after)


def score_grads_body(h, *refs):
    qg, kv, ks, p_ref = refs[0:4], refs[4:8], refs[8], refs[9]
    ds_ref, dq_ref, vs, gs = refs[10:]
    row = lax.broadcasted_iota(jnp.int32, (16, NK), 0)
    for n in range(4):
        vs[0:D, chunk(n)] = kv[n][head(h, 256), :]
        gs[n, 0:D, :] = qg[n][head(h, 256), :]
        gs[n, D:D + 16, :] = qg[n][512:528, :]
    vs[D:D + 16, :] = jnp.where((row >= 3 * h) & (row < 3 * h + 3), -1.0, 0.0).astype(BF)
    for n in range(4):
        pg = dot(gs[n], vs[...], 0, 0)
        ds = (p_ref[h, chunk(n), :].astype(F32) * pg).astype(BF)
        ds_ref[chunk(n), :] = ds
        for group, cols in enumerate(GROUPS):
            dq_ref[group, chunk(n), :] = dot(ds[:, cols], ks[h, 0:D, cols], 1, 1)


def score_grads(h, qg, kv, ks, p):
    return pl.pallas_call(
        lambda *refs: score_grads_body(h, *refs),
        in_specs=[VM] * 10,
        out_specs=[VM] * 2,
        out_shape=[pltpu.VMEM((NQ, NK), BF), pltpu.VMEM((2, NQ, D), F32)],
        scratch_shapes=[
            pltpu.VMEM((D + 16, NK), BF),
            pltpu.VMEM((4, D + 16, R), BF),
        ],
        compiler_params=PARAMS,
        name="score_grads",
    )(*qg, *kv, ks, p)


def key_part(out, xs, ds, p_ref, cols):
    for h in range(2):
        out[head(h), :] = dot(xs[h, 0], ds[h][:, cols], 1, 0).astype(out.dtype)
        out[head(h, 256), :] = dot(xs[h, 1], p_ref[h, :, cols], 1, 0).astype(out.dtype)


def scaled_rows(xs, qg, f):
    for h in range(2):
        for n in range(4):
            fn = f[h:h + 1, chunk(n)]
            xs[h, 0, :, chunk(n)] = (qg[n][head(h), :].astype(F32) * (fn * SCALE)).astype(BF)
            xs[h, 1, :, chunk(n)] = (qg[n][head(h, 256), :].astype(F32) * fn).astype(BF)


def prior_partner_body(*refs):
    qg, st, pair, other, p_ref, ds, dqs = refs[0:4], *refs[4:8], refs[8:10], refs[10:12]
    out, f_ref, near, far, xs = refs[12:]
    top, total = merged(pair[...], other[...], 2)
    f = [jnp.exp2(st[4 * group:4 * group + 2] - top) / total for group in range(2)]
    f_ref[0:2] = f[0]
    f_ref[2:8] = jnp.zeros((6, NQ), F32)
    scaled_rows(xs, qg, f[1])
    key_part(out, xs, ds, p_ref, chunk(3))
    out[512:528] = jnp.zeros((16, R), BF)
    cols = (jnp.concatenate([*f, jnp.zeros((4, NQ), F32)], axis=0) * SCALE).T
    for n in range(4):
        rows = chunk(n)
        for h, dq in enumerate(dqs):
            total = dq[0, rows] * cols[rows, h:h + 1] + dq[1, rows] * cols[rows, 2 + h:3 + h]
            if n < 2:
                near[chunk(n), head(h)] = total
            else:
                far[chunk(n - 2), head(h)] = total.astype(BF)


def prior_partner(qg, st, pair, other, p, ds, dq):
    return pl.pallas_call(
        prior_partner_body,
        in_specs=[VM] * 12,
        out_specs=[VM] * 4,
        out_shape=[
            pltpu.VMEM((528, R), BF),
            pltpu.VMEM((8, NQ), F32),
            pltpu.VMEM((2 * R, 2 * D), F32),
            pltpu.VMEM((2 * R, 2 * D), BF),
        ],
        scratch_shapes=[pltpu.VMEM((2, 2, D, NQ), BF)],
        compiler_params=PARAMS,
        name="prior_partner",
    )(*qg, st, pair, other, p, *ds, *dq)


def key_grads_body(*refs):
    qg, f_ref, p_ref, ds = refs[0:4], refs[4], refs[5], refs[6:8]
    own_partner, prior, own, xs = refs[8:]
    scaled_rows(xs, qg, f_ref[0:2])
    key_part(own_partner, xs, ds, p_ref, chunk(1))
    key_part(prior, xs, ds, p_ref, chunk(2))
    key_part(own, xs, ds, p_ref, chunk(0))


def key_grads(qg, f, p, ds):
    part = pltpu.VMEM((512, R), F32)
    return pl.pallas_call(
        key_grads_body,
        in_specs=[VM] * 8,
        out_specs=[VM] * 3,
        out_shape=[pltpu.VMEM((512, R), BF), part, part],
        scratch_shapes=[pltpu.VMEM((2, 2, D, NQ), BF)],
        compiler_params=PARAMS,
        name="key_grads",
    )(*qg, f, p, *ds)


def middle_sums_body(prior, part, near, far, out, own, pair):
    out[...] = (prior[...] + part[0:512].astype(F32)).astype(BF)
    own[...] = near[chunk(0), :] + far[chunk(0), :].astype(F32)
    pair[...] = (near[chunk(1), :] + far[chunk(1), :].astype(F32)).astype(BF)


def middle_sums(prior, part, near, far):
    return pl.pallas_call(
        middle_sums_body,
        in_specs=[VM] * 4,
        out_specs=[VM] * 3,
        out_shape=[pltpu.VMEM((512, R), BF), pltpu.VMEM((R, 2 * D), F32), pltpu.VMEM((R, 2 * D), BF)],
        compiler_params=PARAMS,
        name="middle_sums",
    )(prior, part, near, far)


def query_sum_body(own, pair, after, out):
    out[...] = (own[...] + pair[...].astype(F32)).astype(BF)


def query_sum(own, pair, after):
    return pl.pallas_call(
        query_sum_body,
        in_specs=[VM] * 3,
        out_shape=jax.ShapeDtypeStruct((R, 2 * D), BF),
        compiler_params=PARAMS,
        cost_estimate=pl.CostEstimate(flops=2 * 10 ** 9, bytes_accessed=0, transcendentals=0),
        name="query_sum",
    )(own, pair, after)


def own_sum_body(own, other, out):
    out[...] = own[...] + other[...].astype(F32)


def own_sum(own, other):
    return pl.pallas_call(
        own_sum_body,
        in_specs=[VM] * 2,
        out_specs=VM,
        out_shape=pltpu.VMEM((512, R), F32),
        compiler_params=PARAMS,
        cost_estimate=pl.CostEstimate(flops=8 * 10 ** 9, bytes_accessed=0, transcendentals=0),
        name="own_sum",
    )(own, other)


def key_sum_body(own, back, dk, dv, done):
    done[...] = jnp.zeros((8, D), F32)
    total = own[...] + back[...].astype(F32)
    dk[...] = total[0:256].T.astype(BF)
    dv[...] = total[256:512].T.astype(BF)


def key_sum(own, back):
    return pl.pallas_call(
        key_sum_body,
        in_specs=[VM] * 2,
        out_shape=[jax.ShapeDtypeStruct((R, 2 * D), BF)] * 2 + [pltpu.VMEM((8, D), F32)],
        compiler_params=PARAMS,
        name="key_sum",
    )(own, back)


def along_y(value, turn):
    outer, inner = lax.axis_size("outer"), lax.axis_size("inner")
    pairs = [
        (o * inner + i, o * inner + (i ^ (6 if o % 2 == turn else 2))) for o in range(outer) for i in range(inner)
    ]
    return lax.ppermute(value, ("outer", "inner"), pairs)


def along_x(value):
    return lax.ppermute(value, "inner", [(i, i ^ 1) for i in range(8)])


def window_pairs():
    outer, inner = lax.axis_size("outer"), lax.axis_size("inner")
    turn = outer // 2
    return [
        (o * inner + i, (o + 1) % outer * inner + (i ^ 1 if o % turn == turn - 1 else i))
        for o in range(outer)
        for i in range(inner)
    ]


def to_next(value):
    return lax.ppermute(value, ("outer", "inner"), window_pairs())


def to_prior(value):
    return lax.ppermute(value, ("outer", "inner"), [(b, a) for a, b in window_pairs()])


def on_device(queries, key_rows, value_rows, outputs, out_grad):
    kv_own, padded, *rest = pack_keys(key_rows, value_rows, queries, outputs, out_grad)
    qg_own = pack_queries(*rest)
    kv_prior = to_next(padded)
    kv_partner = along_x(kv_own)
    kv = [kv_own, kv_partner, kv_prior, to_next(kv_partner)]
    qg_first = along_y(qg_own, 0)
    qg = [qg_own, qg_first, along_y(qg_own, 1), along_y(qg_first, 1)]
    p, st, ks = first_scores(qg, kv)
    ks = last_keys(kv[3], ks)
    p, st = rest_scores(qg, ks, p, st)
    p, st, both = last_scores(qg[3], ks, p, st)
    both_pair = along_y(both, 0)
    ds0, dq0 = score_grads(0, qg, kv, ks, p)
    pair = merge(both, both_pair, dq0)
    pair_other = along_y(pair, 1)
    ds1, dq1 = score_grads(1, qg, kv, ks, p)
    ds, dq = (ds0, ds1), (dq0, dq1)
    part, f, near, far = prior_partner(qg, st, pair, pair_other, p, ds, dq)
    part = along_x(part)
    far = along_y(far, 1)
    own_partner, prior, own = key_grads(qg, f, p, ds)
    other = along_x(own_partner)
    prior, near, pair = middle_sums(prior, part, near, far)
    back = to_prior(prior)
    pair = along_y(pair, 0)
    key_grad, value_grad, done = key_sum(own_sum(own, other), back)
    query_grad = query_sum(near, pair, done)
    return query_grad, key_grad, value_grad


def solution(mesh):
    spec = P(("outer", "inner"), None)
    return jax.shard_map(
        on_device, mesh=mesh, in_specs=(spec,) * 5, out_specs=(spec,) * 3, check_vma=False
    )
```

```python
import jax
import jax.numpy as jnp
from jax import lax
from jax.experimental import pallas as pl
from jax.experimental.pallas import tpu as pltpu
from jax.sharding import PartitionSpec as P

R = 384
D = 128
SCALE = D ** -0.5
C = SCALE * 1.4426950408889634
NQ = 4 * R
NK = 4 * R
GROUPS = (slice(0, 3 * R), slice(3 * R, NK))
F32 = jnp.float32
BF = jnp.bfloat16
VM = pl.BlockSpec(memory_space=pltpu.VMEM)
HBM = pl.BlockSpec(memory_space=pltpu.HBM)
PARAMS = pltpu.CompilerParams(vmem_limit_bytes=16 * 1024 * 1024)
ALONE = pltpu.CompilerParams(vmem_limit_bytes=60 * 1024 * 1024)


def dot(a, b, ca, cb):
    return lax.dot_general(a, b, (((ca,), (cb,)), ((), ())), preferred_element_type=F32)


def chunk(n):
    return slice(n * R, (n + 1) * R)


def head(h, base=0):
    return slice(base + h * D, base + (h + 1) * D)


def turned(ref):
    return ref[...].astype(F32).T


def pack_keys_body(k, v, q, o, g, kv, padded, qs, os, gs, ks, vs, sems):
    copies = [
        pltpu.make_async_copy(src, dst, sems.at[n])
        for n, (src, dst) in enumerate(((k, ks), (v, vs), (q, qs), (o, os), (g, gs)))
    ]
    for copy in copies:
        copy.start()
    copies[0].wait()
    kv[0:256] = turned(ks).astype(BF)
    copies[1].wait()
    kv[256:512] = turned(vs).astype(BF)
    padded[0:512] = kv[...]
    padded[512:544] = jnp.zeros((32, R), BF)
    for copy in copies[2:]:
        copy.wait()


def pack_keys(k, v, q, o, g):
    return pl.pallas_call(
        pack_keys_body,
        in_specs=[HBM] * 5,
        out_specs=[VM] * 5,
        out_shape=[pltpu.VMEM((512, R), BF), pltpu.VMEM((544, R), BF)] + [pltpu.VMEM((R, 2 * D), BF)] * 3,
        scratch_shapes=[pltpu.VMEM((R, 2 * D), BF)] * 2 + [pltpu.SemaphoreType.DMA((5,))],
        compiler_params=ALONE,
        name="pack_keys",
    )(k, v, q, o, g)


def pack_queries_body(q, o, g, qg):
    qg[0:256] = turned(q).astype(BF)
    grads = turned(g)
    qg[256:512] = grads.astype(BF)
    prod = grads * turned(o)
    rows = []
    for h in range(2):
        d = jnp.sum(prod[head(h)], axis=0, keepdims=True)
        hi = d.astype(BF).astype(F32)
        mid = (d - hi).astype(BF).astype(F32)
        rows += [hi, mid, d - hi - mid]
    qg[512:528] = jnp.concatenate(rows + [jnp.zeros((10, R), F32)], axis=0).astype(BF)


def pack_queries(q, o, g):
    return pl.pallas_call(
        pack_queries_body,
        in_specs=[VM] * 3,
        out_specs=VM,
        out_shape=pltpu.VMEM((528, R), BF),
        compiler_params=PARAMS,
        name="pack_queries",
    )(q, o, g)


def score_tile(n, h, q, ks, group, cols, p_ref, st):
    scaled = q[head(h), :].astype(F32) * C
    high = scaled.astype(BF)
    low = (scaled - high.astype(F32)).astype(BF)
    s = dot(jnp.concatenate([high, low], axis=0), ks[h, :, cols], 0, 0)
    m = jnp.max(s, axis=1, keepdims=True)
    p = jnp.exp2(s - m)
    at = 4 * group + h
    st[n, :, at:at + 1] = m
    st[n, :, at + 2:at + 3] = jnp.sum(p, axis=1, keepdims=True)
    p_ref[h, chunk(n), cols] = p.astype(BF)
    return m


def lay_keys(ks, n, ref):
    for h in range(2):
        ks[h, 0:D, chunk(n)] = ref[head(h), :]
        ks[h, D:2 * D, chunk(n)] = ref[head(h), :]


def first_scores_body(own, first, second, k0, k1, k2, p_ref, st_ref, ks, st):
    for n, ref in enumerate((k0, k1, k2)):
        lay_keys(ks, n, ref)
    for n, q in enumerate((own, first, second)):
        for h in range(2):
            score_tile(n, h, q, ks, 0, GROUPS[0], p_ref, st)
        st_ref[0:4, chunk(n)] = st[n].T[0:4, :]


def first_scores(qg, kv):
    return pl.pallas_call(
        first_scores_body,
        in_specs=[VM] * 6,
        out_specs=[VM] * 3,
        out_shape=[pltpu.VMEM((2, NQ, NK), BF), pltpu.VMEM((8, NQ), F32), pltpu.VMEM((2, 2 * D, NK), BF)],
        scratch_shapes=[pltpu.VMEM((3, R, D), F32)],
        compiler_params=PARAMS,
        cost_estimate=pl.CostEstimate(flops=15 * 10 ** 8, bytes_accessed=0, transcendentals=0),
        name="first_scores",
    )(*qg[0:3], *kv[0:3])


def last_keys_body(k3, ks_in, ks):
    lay_keys(ks, 3, k3)


def last_keys(k3, ks):
    return pl.pallas_call(
        last_keys_body,
        in_specs=[VM] * 2,
        out_specs=VM,
        out_shape=pltpu.VMEM((2, 2 * D, NK), BF),
        input_output_aliases={1: 0},
        compiler_params=PARAMS,
        cost_estimate=pl.CostEstimate(flops=10 * 10 ** 8, bytes_accessed=0, transcendentals=0),
        name="last_keys",
    )(k3, ks)


def rest_scores_body(own, first, second, ks, p_in, st_in, p_ref, st_ref, st):
    rows = slice(0, 3 * R)
    st_ref[0:4, rows] = st_in[0:4, rows]
    st_ref[:, chunk(3)] = jnp.zeros((8, R), F32)
    for h in range(2):
        scaled = jnp.concatenate([q[head(h), :] for q in (own, first, second)], axis=1).astype(F32) * C
        high = scaled.astype(BF)
        low = (scaled - high.astype(F32)).astype(BF)
        s = dot(jnp.concatenate([high, low], axis=0), ks[h, :, GROUPS[1]], 0, 0)
        m = jnp.max(s, axis=1, keepdims=True)
        p = jnp.exp2(s - m)
        st[:, 4 + h:5 + h] = m
        st[:, 6 + h:7 + h] = jnp.sum(p, axis=1, keepdims=True)
        p_ref[h, rows, GROUPS[1]] = p.astype(BF)
    st_ref[4:8, rows] = st[...].T[4:8, :]


def rest_scores(qg, ks, p, st):
    return pl.pallas_call(
        rest_scores_body,
        in_specs=[VM] * 6,
        out_specs=[VM] * 2,
        out_shape=[pltpu.VMEM((2, NQ, NK), BF), pltpu.VMEM((8, NQ), F32)],
        scratch_shapes=[pltpu.VMEM((3 * R, D), F32)],
        input_output_aliases={4: 0},
        compiler_params=PARAMS,
        cost_estimate=pl.CostEstimate(flops=10 ** 9, bytes_accessed=0, transcendentals=0),
        name="rest_scores",
    )(*qg[0:3], ks, p, st)


def last_scores_body(third, ks, p_in, st_in, p_ref, st_ref, both_ref, st):
    st_ref[:, 0:3 * R] = st_in[:, 0:3 * R]
    for h in range(2):
        m = score_tile(3, h, third, ks, 0, slice(0, NK), p_ref, st)
        st[3, :, 4 + h:5 + h] = m
        st[3, :, 6 + h:7 + h] = jnp.zeros((R, 1), F32)
    st_ref[:, chunk(3)] = st[3].T[0:8, :]
    top, total = combined(st_ref[0:2], st_ref[2:4], st_ref[4:6], st_ref[6:8])
    both_ref[0:2] = top
    both_ref[2:4] = total
    both_ref[4:8] = jnp.zeros((4, NQ), F32)


def last_scores(third, ks, p, st):
    return pl.pallas_call(
        last_scores_body,
        in_specs=[VM] * 4,
        out_specs=[VM] * 3,
        out_shape=[pltpu.VMEM((2, NQ, NK), BF), pltpu.VMEM((8, NQ), F32), pltpu.VMEM((8, NQ), F32)],
        scratch_shapes=[pltpu.VMEM((4, R, D), F32)],
        input_output_aliases={2: 0},
        compiler_params=PARAMS,
        cost_estimate=pl.CostEstimate(flops=10 ** 9, bytes_accessed=0, transcendentals=0),
        name="last_scores",
    )(third, ks, p, st)


def combined(m0, l0, m1, l1):
    top = jnp.maximum(m0, m1)
    return top, l0 * jnp.exp2(m0 - top) + l1 * jnp.exp2(m1 - top)


def merged(a, b, m):
    b = jnp.concatenate([b[0:4, chunk(n ^ m)] for n in range(4)], axis=1)
    return combined(a[0:2], a[2:4], b[0:2], b[2:4])


def merge_body(a, b, after, out):
    top, total = merged(a[...], b[...], 1)
    out[0:2] = top
    out[2:4] = total
    out[4:8] = jnp.zeros((4, NQ), F32)


def merge(a, b, after):
    return pl.pallas_call(
        merge_body,
        in_specs=[VM] * 3,
        out_specs=VM,
        out_shape=pltpu.VMEM((8, NQ), F32),
        compiler_params=PARAMS,
        name="merge",
    )(a, b, after)


def score_grads_body(h, *refs):
    qg, kv, ks, p_ref = refs[0:4], refs[4:8], refs[8], refs[9]
    ds_ref, dq_ref, vs, gs = refs[10:]
    row = lax.broadcasted_iota(jnp.int32, (16, NK), 0)
    for n in range(4):
        vs[0:D, chunk(n)] = kv[n][head(h, 256), :]
        gs[n, 0:D, :] = qg[n][head(h, 256), :]
        gs[n, D:D + 16, :] = qg[n][512:528, :]
    vs[D:D + 16, :] = jnp.where((row >= 3 * h) & (row < 3 * h + 3), -1.0, 0.0).astype(BF)
    for n in range(4):
        pg = dot(gs[n], vs[...], 0, 0)
        ds = (p_ref[h, chunk(n), :].astype(F32) * pg).astype(BF)
        ds_ref[chunk(n), :] = ds
        for group, cols in enumerate(GROUPS):
            dq_ref[group, chunk(n), :] = dot(ds[:, cols], ks[h, 0:D, cols], 1, 1)


def score_grads(h, qg, kv, ks, p):
    return pl.pallas_call(
        lambda *refs: score_grads_body(h, *refs),
        in_specs=[VM] * 10,
        out_specs=[VM] * 2,
        out_shape=[pltpu.VMEM((NQ, NK), BF), pltpu.VMEM((2, NQ, D), F32)],
        scratch_shapes=[
            pltpu.VMEM((D + 16, NK), BF),
            pltpu.VMEM((4, D + 16, R), BF),
        ],
        compiler_params=PARAMS,
        name="score_grads",
    )(*qg, *kv, ks, p)


def key_part(out, xs, ds, p_ref, cols):
    for h in range(2):
        out[head(h), :] = dot(xs[h, 0], ds[h][:, cols], 1, 0).astype(out.dtype)
        out[head(h, 256), :] = dot(xs[h, 1], p_ref[h, :, cols], 1, 0).astype(out.dtype)


def scaled_rows(xs, qg, f):
    for h in range(2):
        for n in range(4):
            fn = f[h:h + 1, chunk(n)]
            xs[h, 0, :, chunk(n)] = (qg[n][head(h), :].astype(F32) * (fn * SCALE)).astype(BF)
            xs[h, 1, :, chunk(n)] = (qg[n][head(h, 256), :].astype(F32) * fn).astype(BF)


def prior_partner_body(*refs):
    qg, st, pair, other, p_ref, ds, dqs = refs[0:4], *refs[4:8], refs[8:10], refs[10:12]
    out, f_ref, near, far, xs = refs[12:]
    top, total = merged(pair[...], other[...], 2)
    f = [jnp.exp2(st[4 * group:4 * group + 2] - top) / total for group in range(2)]
    f_ref[0:2] = f[0]
    f_ref[2:8] = jnp.zeros((6, NQ), F32)
    scaled_rows(xs, qg, f[1])
    key_part(out, xs, ds, p_ref, chunk(3))
    out[512:528] = jnp.zeros((16, R), BF)
    cols = (jnp.concatenate([*f, jnp.zeros((4, NQ), F32)], axis=0) * SCALE).T
    for n in range(4):
        rows = chunk(n)
        for h, dq in enumerate(dqs):
            total = dq[0, rows] * cols[rows, h:h + 1] + dq[1, rows] * cols[rows, 2 + h:3 + h]
            if n < 2:
                near[chunk(n), head(h)] = total
            else:
                far[chunk(n - 2), head(h)] = total.astype(BF)


def prior_partner(qg, st, pair, other, p, ds, dq):
    return pl.pallas_call(
        prior_partner_body,
        in_specs=[VM] * 12,
        out_specs=[VM] * 4,
        out_shape=[
            pltpu.VMEM((528, R), BF),
            pltpu.VMEM((8, NQ), F32),
            pltpu.VMEM((2 * R, 2 * D), F32),
            pltpu.VMEM((2 * R, 2 * D), BF),
        ],
        scratch_shapes=[pltpu.VMEM((2, 2, D, NQ), BF)],
        compiler_params=PARAMS,
        name="prior_partner",
    )(*qg, st, pair, other, p, *ds, *dq)


def key_grads_body(*refs):
    qg, f_ref, p_ref, ds = refs[0:4], refs[4], refs[5], refs[6:8]
    own_partner, prior, own, xs = refs[8:]
    scaled_rows(xs, qg, f_ref[0:2])
    key_part(own_partner, xs, ds, p_ref, chunk(1))
    key_part(prior, xs, ds, p_ref, chunk(2))
    key_part(own, xs, ds, p_ref, chunk(0))


def key_grads(qg, f, p, ds):
    part = pltpu.VMEM((512, R), F32)
    return pl.pallas_call(
        key_grads_body,
        in_specs=[VM] * 8,
        out_specs=[VM] * 3,
        out_shape=[pltpu.VMEM((512, R), BF), part, part],
        scratch_shapes=[pltpu.VMEM((2, 2, D, NQ), BF)],
        compiler_params=PARAMS,
        name="key_grads",
    )(*qg, f, p, *ds)


def middle_sums_body(prior, part, near, far, out, own, pair):
    out[...] = (prior[...] + part[0:512].astype(F32)).astype(BF)
    own[...] = near[chunk(0), :] + far[chunk(0), :].astype(F32)
    pair[...] = (near[chunk(1), :] + far[chunk(1), :].astype(F32)).astype(BF)


def middle_sums(prior, part, near, far):
    return pl.pallas_call(
        middle_sums_body,
        in_specs=[VM] * 4,
        out_specs=[VM] * 3,
        out_shape=[pltpu.VMEM((512, R), BF), pltpu.VMEM((R, 2 * D), F32), pltpu.VMEM((R, 2 * D), BF)],
        compiler_params=PARAMS,
        name="middle_sums",
    )(prior, part, near, far)


def query_sum_body(own, pair, after, out):
    out[...] = (own[...] + pair[...].astype(F32)).astype(BF)


def query_sum(own, pair, after):
    return pl.pallas_call(
        query_sum_body,
        in_specs=[VM] * 3,
        out_shape=jax.ShapeDtypeStruct((R, 2 * D), BF),
        compiler_params=PARAMS,
        cost_estimate=pl.CostEstimate(flops=2 * 10 ** 9, bytes_accessed=0, transcendentals=0),
        name="query_sum",
    )(own, pair, after)


def own_sum_body(own, other, out):
    out[...] = own[...] + other[...].astype(F32)


def own_sum(own, other):
    return pl.pallas_call(
        own_sum_body,
        in_specs=[VM] * 2,
        out_specs=VM,
        out_shape=pltpu.VMEM((512, R), F32),
        compiler_params=PARAMS,
        cost_estimate=pl.CostEstimate(flops=8 * 10 ** 9, bytes_accessed=0, transcendentals=0),
        name="own_sum",
    )(own, other)


def key_sum_body(own, back, dk, dv, done):
    done[...] = jnp.zeros((8, D), F32)
    total = own[...] + back[...].astype(F32)
    dk[...] = total[0:256].T.astype(BF)
    dv[...] = total[256:512].T.astype(BF)


def key_sum(own, back):
    return pl.pallas_call(
        key_sum_body,
        in_specs=[VM] * 2,
        out_shape=[jax.ShapeDtypeStruct((R, 2 * D), BF)] * 2 + [pltpu.VMEM((8, D), F32)],
        compiler_params=PARAMS,
        name="key_sum",
    )(own, back)


def along_y(value, turn):
    outer, inner = lax.axis_size("outer"), lax.axis_size("inner")
    pairs = [
        (o * inner + i, o * inner + (i ^ (6 if o % 2 == turn else 2))) for o in range(outer) for i in range(inner)
    ]
    return lax.ppermute(value, ("outer", "inner"), pairs)


def along_x(value):
    return lax.ppermute(value, "inner", [(i, i ^ 1) for i in range(8)])


def window_pairs():
    outer, inner = lax.axis_size("outer"), lax.axis_size("inner")
    turn = outer // 2
    return [
        (o * inner + i, (o + 1) % outer * inner + (i ^ 1 if o % turn == turn - 1 else i))
        for o in range(outer)
        for i in range(inner)
    ]


def to_next(value):
    return lax.ppermute(value, ("outer", "inner"), window_pairs())


def to_prior(value):
    return lax.ppermute(value, ("outer", "inner"), [(b, a) for a, b in window_pairs()])


def on_device(queries, key_rows, value_rows, outputs, out_grad):
    kv_own, padded, *rest = pack_keys(key_rows, value_rows, queries, outputs, out_grad)
    qg_own = pack_queries(*rest)
    kv_prior = to_next(padded)
    kv_partner = along_x(kv_own)
    kv = [kv_own, kv_partner, kv_prior, to_next(kv_partner)]
    qg_first = along_y(qg_own, 0)
    qg = [qg_own, qg_first, along_y(qg_own, 1), along_y(qg_first, 1)]
    p, st, ks = first_scores(qg, kv)
    ks = last_keys(kv[3], ks)
    p, st = rest_scores(qg, ks, p, st)
    p, st, both = last_scores(qg[3], ks, p, st)
    both_pair = along_y(both, 0)
    ds0, dq0 = score_grads(0, qg, kv, ks, p)
    pair = merge(both, both_pair, dq0)
    pair_other = along_y(pair, 1)
    ds1, dq1 = score_grads(1, qg, kv, ks, p)
    ds, dq = (ds0, ds1), (dq0, dq1)
    part, f, near, far = prior_partner(qg, st, pair, pair_other, p, ds, dq)
    part = along_x(part)
    far = along_y(far, 1)
    own_partner, prior, own = key_grads(qg, f, p, ds)
    other = along_x(own_partner)
    prior, near, pair = middle_sums(prior, part, near, far)
    back = to_prior(prior)
    pair = along_y(pair, 0)
    key_grad, value_grad, done = key_sum(own_sum(own, other), back)
    query_grad = query_sum(near, pair, done)
    return query_grad, key_grad, value_grad


def solution(mesh):
    spec = P(("outer", "inner"), None)
    return jax.shard_map(
        on_device, mesh=mesh, in_specs=(spec,) * 5, out_specs=(spec,) * 3, check_vma=False
    )
```
